128 devices in a mesh: morton: 32 (over y, x, core), level: 4 (over z).
Axes of the slice: x: 4, y: 4, z: 4, core: 2. Of those that a mesh axis runs over, the one named last changes fastest.
Arguments:
- coef: float32 [131072, 512], P(('morton', 'level')), may hold values from -6 to 6
- mask: int32 [131072], P(('morton', 'level')), may hold values from 0 to 1, as said below
- neighbours: int32 [131072, 2], P(('morton', 'level')), may hold values from -1 to 131071, as said below
- two_scale: float32 [16, 16], replicated, may hold values from -1.5 to 1.5
- deriv_blocks: float32 [3, 8, 8], replicated, may hold values from -1.25 to 1.25
Outputs:
- wavelet_coef: float32 [131072, 512], P(('morton', 'level'))
- derivative: float32 [131072, 512], P(('morton', 'level'))
The draws below stay inside these ranges and needn't reach their ends.
Inputs may be any that keep to these rules, and one draw needn't show every extreme that they name: `mask`: aligned groups of 8 boxes (families) share one value; in each aligned tile of 128 boxes the live families come first, and half of them or more are live. `neighbours`: device ranks follow box indices in blocks of 1024. An entry on its box's own device is the box just before (left) or after (right) it, or -1 at the device's first or last box. Of the 2048 entries of one device's boxes, at most 8 lie on any one other device, exactly 8 on some other device, and they lie on exactly 127 other devices.
All inputs are finite; a program needn't handle non-finite values.
Results may differ from the reference program's by a relative error of at most 0.0003.
Values sent between devices are 32-bit elements; how exact they have to be, the bound alone decides.
No kernel may reach another device: no remote copies, remote signals or barrier semaphores. Data moves between devices by JAX's collectives and lax.ppermute only.
A program may use at most 192 MiB of HBM per device.

```python
import jax
import jax.numpy as jnp
from jax import lax

ORDER = 8
COEFS = 512
LEAF_DEV = 1024
TILE = 128
CAP = 8
PEERS = 127
LEAF = 131072


def draw_mask(key, part):
    key = jax.random.fold_in(key, 5)
    tiles = LEAF // TILE
    live_families = jax.random.randint(key, (tiles, 1), TILE // 16, TILE // 8 + 1)
    family_ids = jnp.arange(TILE // 8)[None, :]
    flags = (family_ids < live_families).astype(jnp.int32)
    return jnp.repeat(flags, 8, axis=1).reshape(LEAF).astype(jnp.int32)


def draw_neighbours(key, part):
    key = jax.random.fold_in(key, 11)
    key_counts, key_order, key_peers, key_rows = jax.random.split(key, 4)
    device_count = LEAF // LEAF_DEV
    entries = 2 * LEAF_DEV
    devices = jnp.arange(device_count)
    counts = jax.random.randint(key_counts, (device_count, PEERS), 1, CAP + 1)
    counts = counts.at[:, 0].set(CAP)
    ends = jnp.cumsum(counts, axis=1)
    ranking = jax.vmap(lambda sub_key: jax.random.permutation(sub_key, entries))(jax.random.split(key_order, device_count))
    is_remote = ranking < ends[:, -1:]
    peer_slot = jax.vmap(lambda bounds, values: jnp.searchsorted(bounds, values, side='right'))(ends, ranking)
    peer_slot = jnp.clip(peer_slot, 0, PEERS - 1)
    offsets = jax.vmap(lambda sub_key: jax.random.permutation(sub_key, device_count - 1)[:PEERS] + 1)(jax.random.split(key_peers, device_count))
    chosen = jnp.take_along_axis(offsets, peer_slot, axis=1)
    target_device = (devices[:, None] + chosen) % device_count
    far_rows = jax.random.randint(key_rows, (device_count, entries), 0, LEAF_DEV)
    entry_ids = jnp.arange(entries)[None, :]
    local_rows = entry_ids // 2 - 1 + 2 * (entry_ids % 2)
    local_index = jnp.where((local_rows >= 0) & (local_rows < LEAF_DEV), devices[:, None] * LEAF_DEV + local_rows, -1)
    result = jnp.where(is_remote, target_device * LEAF_DEV + far_rows, local_index)
    return result.reshape(LEAF, 2).astype(jnp.int32)


def steps_of(own_key, extent, cuts, least, top_value):
    loudness = 1.0
    for position, blocks in cuts:
        steps = jax.random.uniform(jax.random.fold_in(jax.random.fold_in(own_key, 6), position), (blocks,), jnp.float32, least / len(cuts), top_value / len(cuts))
        loudness = loudness * jnp.repeat(jnp.exp(steps), extent[position] // blocks).reshape((-1,) + (1,) * (len(extent) - 1 - position))
    return loudness


def normal_values(rng, dims, width, bound, shards=(), held_as=jnp.bfloat16):
    values = jax.random.normal(rng, dims, jnp.float32) * width
    if len(shards) > 0:
        values = steps_of(rng, dims, shards, -0.22, 0.18) * values
    return jnp.clip(values, min=-bound, max=bound).astype(held_as)


def setup_inputs(seed: int = 0) -> dict:
    keys = jax.random.split(jax.random.key(seed), 6)
    coef = normal_values(keys[0], (LEAF, COEFS), 1.0, 6.0, ((0, 128),), jnp.float32)
    mask = draw_mask(jax.random.fold_in(keys[5], 71), 0)
    neighbours = draw_neighbours(jax.random.fold_in(keys[5], 71), 0)
    two_scale = normal_values(keys[3], (16, 16), 16 ** -0.5, 1.5, (), jnp.float32)
    deriv_blocks = normal_values(keys[4], (3, ORDER, ORDER), (3 * ORDER) ** -0.5, 1.25, (), jnp.float32)
    return dict(coef=coef, mask=mask, neighbours=neighbours, two_scale=two_scale, deriv_blocks=deriv_blocks)


def compress_block(block, two_scale):
    highest = lax.Precision.HIGHEST
    families = block.shape[0] // 8
    family_cube = block.reshape(families, 2, 2, 2, ORDER, ORDER, ORDER)
    family_cube = family_cube.transpose(0, 1, 4, 2, 5, 3, 6).reshape(families, 16, 16, 16)
    family_cube = jnp.einsum('ia,fabc->fibc', two_scale, family_cube, precision=highest)
    family_cube = jnp.einsum('jb,fibc->fijc', two_scale, family_cube, precision=highest)
    family_cube = jnp.einsum('lc,fijc->fijl', two_scale, family_cube, precision=highest)
    family_cube = family_cube.reshape(families, 2, ORDER, 2, ORDER, 2, ORDER).transpose(0, 1, 3, 5, 2, 4, 6)
    return family_cube.reshape(families * 8, COEFS)


def along_x(block_matrix, values):
    shaped = values.reshape(-1, ORDER, ORDER * ORDER)
    result = jnp.einsum('ia,bak->bik', block_matrix, shaped, precision=lax.Precision.HIGHEST)
    return result.reshape(-1, COEFS)


def reference(coef, mask, neighbours, two_scale, deriv_blocks):
    live_coef = coef * mask[:, None].astype(jnp.float32)
    groups = LEAF // LEAF_DEV

    def fetch(index_column):
        picked = live_coef[jnp.clip(index_column, 0, LEAF - 1)]
        return jnp.where((index_column >= 0)[:, None], picked, jnp.zeros_like(picked))

    def derive(inputs):
        near_index, own_rows, own_mask = inputs
        near_left = fetch(near_index[:, 0])
        near_right = fetch(near_index[:, 1])
        total = along_x(deriv_blocks[0], near_left) + along_x(deriv_blocks[1], own_rows) + along_x(deriv_blocks[2], near_right)
        return total * own_mask[:, None].astype(jnp.float32)

    derivative = lax.map(derive, (neighbours.reshape(groups, LEAF_DEV, 2), live_coef.reshape(groups, LEAF_DEV, COEFS), mask.reshape(groups, LEAF_DEV)))
    wavelet_coef = lax.map(lambda block: compress_block(block, two_scale), derivative)
    return wavelet_coef.reshape(LEAF, COEFS), derivative.reshape(LEAF, COEFS)
```

```python
import jax
import jax.numpy as jnp
from jax import lax
from jax.experimental import pallas as pl
from jax.experimental.pallas import tpu as pltpu
from jax.sharding import PartitionSpec as P

ORDER = 8
COEFS = 512
SQ = ORDER * ORDER
LANES = 128
CHUNKS = COEFS // LANES
TILE = 128
CAP = 8
AXES = ("morton", "level")
F32 = jnp.float32
BF16 = jnp.bfloat16
I32 = jnp.int32


def iota(shape, dim):
    return lax.broadcasted_iota(I32, shape, dim)


def dot(a, b, dims=((1,), (0,))):
    return lax.dot_general(a, b, (dims, ((), ())), preferred_element_type=F32)


def split(x):
    high = x.astype(BF16)
    return high, (x - high.astype(F32)).astype(BF16)


def route_kernel(rank_ref, near_ref, mask_ref, request_ref, ghost_ref, local_ref):
    boxes = near_ref.shape[1]
    peers = request_ref.shape[0]
    part = 256
    rank = rank_ref[0]
    tri_row, tri_col = iota((part, 2 * part), 0), iota((part, 2 * part), 1)
    tri = ((tri_row < tri_col) | (tri_col >= part)).astype(F32).astype(BF16)
    peer_ids = iota((peers, part), 0)
    slot_ids = iota((CAP, part), 0)
    carry = jnp.zeros((peers, part), F32)
    high_sum = jnp.zeros((peers, CAP), F32)
    low_sum = jnp.zeros((peers, CAP), F32)
    for side in range(2):
        for start in range(0, boxes, part):
            span = pl.ds(start, part)
            entry = near_ref[pl.ds(side, 1), span]
            live = mask_ref[:, span] > 0
            owner = lax.shift_right_arithmetic(entry, 10)
            row = lax.bitwise_and(entry, boxes - 1) + side * boxes
            mine = owner == rank
            remote = (owner >= 0) & (~mine) & live
            local_ref[pl.ds(side, 1), span] = (mine & live).astype(F32)
            target = jnp.where(remote, owner, -1)
            hot_mask = peer_ids == target
            hot_f = hot_mask.astype(F32)
            hot = hot_f.astype(BF16)
            counted = dot(hot, tri)
            before = counted[:, :part] + carry
            carry = carry + counted[:, part:]
            slot = jnp.sum(hot_f * before, axis=0, keepdims=True).astype(I32)
            ghost_ref[pl.ds(side, 1), span] = jnp.where(
                remote, owner * CAP + slot, rank * CAP
            )
            picked = slot_ids == slot
            high = lax.shift_right_logical(row, 6).astype(F32)
            low = lax.bitwise_and(row, 63).astype(F32)
            high_sum += dot(hot, jnp.where(picked, high, 0.0).astype(BF16), ((1,), (1,)))
            low_sum += dot(hot, jnp.where(picked, low, 0.0).astype(BF16), ((1,), (1,)))
    request = (high_sum * 64.0 + low_sum).astype(I32)
    request_ref[...] = request.reshape(peers, 1, CAP)


def route(rank, near, mask_row, peers):
    boxes = near.shape[1]
    vmem = pl.BlockSpec(memory_space=pltpu.VMEM)
    return pl.pallas_call(
        route_kernel,
        in_specs=[pl.BlockSpec(memory_space=pltpu.SMEM), vmem, vmem],
        out_specs=[vmem, vmem, vmem],
        out_shape=[
            jax.ShapeDtypeStruct((peers, 1, CAP), I32),
            jax.ShapeDtypeStruct((2, boxes), I32),
            jax.ShapeDtypeStruct((2, boxes), F32),
        ],
        name="route",
    )(rank, near, mask_row)


def fill_weights(blocks_ref, weight_ref, sides):
    first_half = iota((8, LANES), 1) < SQ
    for n, side in enumerate(sides):
        for i in range(CHUNKS):
            for j in range(CHUNKS):
                def at(di, dj):
                    return blocks_ref[side, (2 * i + di) * ORDER + 2 * j + dj]

                k = ((n * CHUNKS + i) * CHUNKS + j) * 2
                weight_ref[k] = jnp.where(first_half, at(0, 0), at(1, 1))
                weight_ref[k + 1] = jnp.where(first_half, at(0, 1), at(1, 0))


def live_count(mask_ref, tile):
    total = jnp.int32(0)
    for family in range(TILE // 8):
        total += mask_ref[tile * TILE + family * 8]
    return total * 8


def apply_blocks(coef_ref, weight_ref, live, count, put, rows=32):
    def step(r, carry):
        start = pl.multiple_of(r * rows, rows)
        alive = (iota((rows, LANES), 0) + start) < live
        straight, swapped = [], []
        for j in range(CHUNKS):
            x = coef_ref[pl.ds(start, rows), pl.ds(j * LANES, LANES)]
            x = jnp.where(alive, x, 0.0)
            straight.append(x.reshape(rows // 8, 8, LANES))
            swapped.append(pltpu.roll(x, SQ, 1).reshape(rows // 8, 8, LANES))
        for n in range(count):
            for i in range(CHUNKS):
                total = None
                for j in range(CHUNKS):
                    k = ((n * CHUNKS + i) * CHUNKS + j) * 2
                    term = (
                        weight_ref[k][None] * straight[j]
                        + weight_ref[k + 1][None] * swapped[j]
                    )
                    total = term if total is None else total + term
                put(n, i, start, total.reshape(rows, LANES))
        return carry

    lax.fori_loop(0, TILE // rows, step, 0)


def table_kernel(mask_ref, blocks_ref, coef_ref, table_ref, weight_ref):
    tile = pl.program_id(0)

    @pl.when(tile == 0)
    def _():
        fill_weights(blocks_ref, weight_ref, (0, 2))

    def put(n, i, start, value):
        rows = value.shape[0]
        table_ref[n, pl.ds(start * CHUNKS + i, rows, stride=CHUNKS), :] = value

    apply_blocks(coef_ref, weight_ref, live_count(mask_ref, tile), 2, put)


def make_table(mask, blocks, coef):
    boxes = coef.shape[0]
    smem = pl.BlockSpec(memory_space=pltpu.SMEM)
    return pl.pallas_call(
        table_kernel,
        grid=(boxes // TILE,),
        in_specs=[smem, smem, pl.BlockSpec((TILE, COEFS), lambda t: (t, 0))],
        out_specs=pl.BlockSpec((2, TILE * CHUNKS, LANES), lambda t: (0, t, 0)),
        out_shape=jax.ShapeDtypeStruct((2, boxes * CHUNKS, LANES), F32),
        scratch_shapes=[pltpu.VMEM((2 * CHUNKS * CHUNKS * 2, 8, LANES), F32)],
        cost_estimate=pl.CostEstimate(
            flops=boxes * COEFS * 32, bytes_accessed=boxes * COEFS * 12, transcendentals=0
        ),
        name="table",
    )(mask, blocks, coef)


def serve_kernel(rank_ref, request_ref, table_ref, reply_ref):
    peers = reply_ref.shape[0] // (CAP * CHUNKS)
    first = pl.program_id(0) * peers

    def step(p, carry):
        for s in range(CAP):
            row = request_ref[first + p, 0, s]
            reply_ref[pl.ds((p * CAP + s) * CHUNKS, CHUNKS), :] = table_ref[
                pl.ds(row * CHUNKS, CHUNKS), :
            ]
        return carry

    lax.fori_loop(0, peers, step, 0, unroll=4)
    own = rank_ref[0] - first

    @pl.when((own >= 0) & (own < peers))
    def _():
        span = CAP * CHUNKS
        reply_ref[pl.ds(pl.multiple_of(own * span, span), span), :] = jnp.zeros(
            (span, LANES), F32
        )


def serve(rank, request, table):
    peers = request.shape[0]
    steps = 4
    smem = pl.BlockSpec(memory_space=pltpu.SMEM)
    return pl.pallas_call(
        serve_kernel,
        grid=(steps,),
        in_specs=[smem, smem, pl.BlockSpec(memory_space=pltpu.VMEM)],
        out_specs=pl.BlockSpec((peers * CAP * CHUNKS // steps, LANES), lambda t: (t, 0)),
        out_shape=jax.ShapeDtypeStruct((peers * CAP * CHUNKS, LANES), F32),
        name="serve",
    )(rank, request, table)


def expand(scale, rows, cols, row_of, col_of):
    pick_row = (iota((rows, 16), 1) == row_of(iota((rows, 16), 0))).astype(F32)
    pick_col = (iota((16, cols), 0) == col_of(iota((16, cols), 1))).astype(F32)
    highest = lax.Precision.HIGHEST
    wide = jnp.dot(pick_row, scale, precision=highest, preferred_element_type=F32)
    return jnp.dot(wide, pick_col, precision=highest, preferred_element_type=F32)


def base_kernel(
    mask_ref, blocks_ref, local_ref, coef_ref, table_ref, scale_ref,
    base_ref, yz_high_ref, yz_low_ref, x_high_ref, x_low_ref, weight_ref,
):
    tile = pl.program_id(0)
    tiles = pl.num_programs(0)
    span = 2 * SQ * 2

    @pl.when(tile == 0)
    def _():
        fill_weights(blocks_ref, weight_ref, (1,))
        scale = scale_ref[...]
        scale_t = scale.T
        def bits(v, shift, mask):
            return lax.bitwise_and(lax.shift_right_logical(v, shift), mask)

        def y_of(v):
            return bits(v, 7, 1) * 8 + bits(v, 3, 7)

        def z_of(v):
            return bits(v, 6, 1) * 8 + bits(v, 0, 7)

        yz = expand(scale_t, span, span, y_of, y_of) * expand(scale_t, span, span, z_of, z_of)
        yz_high_ref[...], yz_low_ref[...] = split(yz)

        def x_of(v):
            return lax.shift_right_logical(v, 4)

        wide = expand(scale, span, span, x_of, x_of)
        same = bits(iota((span, span), 0), 0, 15) == bits(iota((span, span), 1), 0, 15)
        x_high_ref[...], x_low_ref[...] = split(jnp.where(same, wide, 0.0))

    def put(n, i, start, value):
        rows = value.shape[0]
        base_ref[pl.ds(start * CHUNKS + i, rows, stride=CHUNKS), :] = value

    apply_blocks(coef_ref, weight_ref, live_count(mask_ref, tile), 1, put)
    boxes = tiles * TILE

    def add(b, carry):
        box = tile * TILE + b
        spot = pl.ds(b * CHUNKS, CHUNKS)
        left = table_ref[0, pl.ds(jnp.maximum(box - 1, 0) * CHUNKS, CHUNKS), :]
        right = table_ref[1, pl.ds(jnp.minimum(box + 1, boxes - 1) * CHUNKS, CHUNKS), :]
        base_ref[spot, :] += left * local_ref[0, box] + right * local_ref[1, box]
        return carry

    lax.fori_loop(0, TILE, add, 0, unroll=8)


def make_base(mask, blocks, local, coef, table, scale):
    boxes = coef.shape[0]
    span = 4 * SQ
    smem = pl.BlockSpec(memory_space=pltpu.SMEM)
    vmem = pl.BlockSpec(memory_space=pltpu.VMEM)
    return pl.pallas_call(
        base_kernel,
        grid=(boxes // TILE,),
        in_specs=[
            smem, smem, smem,
            pl.BlockSpec((TILE, COEFS), lambda t: (t, 0)),
            vmem, vmem,
        ],
        out_specs=[pl.BlockSpec((TILE * CHUNKS, LANES), lambda t: (t, 0)), vmem, vmem, vmem, vmem],
        out_shape=[jax.ShapeDtypeStruct((boxes * CHUNKS, LANES), F32)]
        + [jax.ShapeDtypeStruct((span, span), BF16)] * 4,
        scratch_shapes=[pltpu.VMEM((CHUNKS * CHUNKS * 2, 8, LANES), F32)],
        cost_estimate=pl.CostEstimate(
            flops=boxes * COEFS * 32, bytes_accessed=boxes * COEFS * 16, transcendentals=0
        ),
        name="base",
    )(mask, blocks, local, coef, table, scale)


def product(left, right):
    left_high, left_low = left
    right_high, right_low = right
    return (
        dot(left_high, right_high) + dot(left_low, right_high) + dot(left_high, right_low)
    )


def final_kernel(
    ghost_index_ref, ghosts_ref, base_ref, yz_high_ref, yz_low_ref, x_high_ref, x_low_ref,
    wavelet_ref, derivative_ref, rows_ref, in_high_ref, in_low_ref, out_ref,
):
    tile = pl.program_id(0)
    families = TILE // 8

    def add(b, carry):
        box = tile * TILE + b
        spot = pl.ds(b * CHUNKS, CHUNKS)
        left = ghosts_ref[pl.ds(ghost_index_ref[0, box] * CHUNKS, CHUNKS), :]
        right = ghosts_ref[pl.ds(ghost_index_ref[1, box] * CHUNKS, CHUNKS), :]
        rows_ref[spot, :] = base_ref[spot, :] + (left + right)
        return carry

    lax.fori_loop(0, TILE, add, 0, unroll=8)
    for j in range(CHUNKS):
        derivative_ref[:, pl.ds(j * LANES, LANES)] = rows_ref[pl.ds(j, TILE, stride=CHUNKS), :]
    first_half = iota((families, LANES), 1) < SQ
    for cx in range(2):
        for j in range(CHUNKS):
            for cy in range(2):
                box = cx * 4 + cy * 2
                z0 = rows_ref[pl.ds(box * CHUNKS + j, families, stride=8 * CHUNKS), :]
                z1 = rows_ref[pl.ds((box + 1) * CHUNKS + j, families, stride=8 * CHUNKS), :]
                even = jnp.where(first_half, z0, pltpu.roll(z1, SQ, 1))
                odd = jnp.where(first_half, pltpu.roll(z0, SQ, 1), z1)
                for half, value in enumerate((even, odd)):
                    spot = pl.ds((cx * 8 + 2 * j + half) * families, families)
                    lanes = pl.ds(cy * LANES, LANES)
                    high, low = split(value)
                    in_high_ref[spot, lanes] = high
                    in_low_ref[spot, lanes] = low
    middle = product(
        (in_high_ref[...], in_low_ref[...]), (yz_high_ref[...], yz_low_ref[...])
    )
    result = product((x_high_ref[...], x_low_ref[...]), split(middle))
    for ox in range(2):
        for i in range(CHUNKS):
            for oy in range(2):
                top = (ox * 8 + 2 * i) * families
                lanes = slice(oy * LANES, (oy + 1) * LANES)
                even = result[top : top + families, lanes]
                odd = result[top + families : top + 2 * families, lanes]
                z0 = jnp.where(first_half, even, pltpu.roll(odd, SQ, 1))
                z1 = jnp.where(first_half, pltpu.roll(even, SQ, 1), odd)
                box = ox * 4 + oy * 2
                out_ref[i, pl.ds(box, families, stride=8), :] = z0
                out_ref[i, pl.ds(box + 1, families, stride=8), :] = z1
    for i in range(CHUNKS):
        wavelet_ref[:, pl.ds(i * LANES, LANES)] = out_ref[i]


def finish(ghost_index, ghosts, base, matrices):
    boxes = ghost_index.shape[1]
    span = 4 * SQ
    vmem = pl.BlockSpec(memory_space=pltpu.VMEM)
    block = pl.BlockSpec((TILE, COEFS), lambda t: (t, 0))
    return pl.pallas_call(
        final_kernel,
        grid=(boxes // TILE,),
        in_specs=[
            pl.BlockSpec(memory_space=pltpu.SMEM),
            vmem,
            pl.BlockSpec((TILE * CHUNKS, LANES), lambda t: (t, 0)),
            vmem, vmem, vmem, vmem,
        ],
        out_specs=[block, block],
        out_shape=[jax.ShapeDtypeStruct((boxes, COEFS), F32)] * 2,
        scratch_shapes=[
            pltpu.VMEM((TILE * CHUNKS, LANES), F32),
            pltpu.VMEM((span, span), BF16),
            pltpu.VMEM((span, span), BF16),
            pltpu.VMEM((CHUNKS, TILE, LANES), F32),
        ],
        name="finish",
    )(ghost_index, ghosts, base, *matrices)


def exchange(x):
    return lax.all_to_all(x, AXES, split_axis=0, concat_axis=0, tiled=True)


def body(coef, mask, neighbours, two_scale, deriv_blocks):
    boxes = coef.shape[0]
    rank = lax.axis_index(AXES).astype(I32).reshape(1)
    peers = lax.axis_size("morton") * lax.axis_size("level")
    blocks = deriv_blocks.reshape(3, SQ)
    request, ghost_index, local = route(rank, neighbours.T, mask.reshape(1, boxes), peers)
    asked = exchange(request)
    table = make_table(mask, blocks, coef)
    reply = serve(rank, asked, table.reshape(2 * boxes * CHUNKS, LANES))
    ghosts = exchange(reply.reshape(peers, CAP * CHUNKS, LANES))
    base, *matrices = make_base(mask, blocks, local, coef, table, two_scale)
    return tuple(finish(ghost_index, ghosts.reshape(-1, LANES), base, matrices))


def solution(mesh):
    in_specs = (P(AXES, None), P(AXES), P(AXES, None), P(), P())
    out_specs = (P(AXES, None), P(AXES, None))
    return jax.shard_map(body, mesh=mesh, in_specs=in_specs, out_specs=out_specs, check_vma=False)
```

```python
import jax
import jax.numpy as jnp
from jax import lax
from jax.experimental import pallas as pl
from jax.experimental.pallas import tpu as pltpu
from jax.sharding import PartitionSpec as P

ORDER = 8
COEFS = 512
SQ = ORDER * ORDER
LANES = 128
CHUNKS = COEFS // LANES
TILE = 128
CAP = 8
EARLY = 4
AXES = ("morton", "level")
F32 = jnp.float32
BF16 = jnp.bfloat16
I32 = jnp.int32
LIMIT = pltpu.CompilerParams(vmem_limit_bytes=24 * 1024 * 1024)
ANYWHERE = pl.BlockSpec(memory_space=pl.ANY)
VMEM_SPEC = pl.BlockSpec(memory_space=pltpu.VMEM)
SMEM_SPEC = pl.BlockSpec(memory_space=pltpu.SMEM)


def in_hbm(*arrays):
    return [pltpu.with_memory_space_constraint(x, pltpu.HBM) for x in arrays]


def iota(shape, dim):
    return lax.broadcasted_iota(I32, shape, dim)


def dot(a, b, dims=((1,), (0,))):
    return lax.dot_general(a, b, (dims, ((), ())), preferred_element_type=F32)


def split(x):
    high = x.astype(BF16)
    return high, (x - high.astype(F32)).astype(BF16)


def route_kernel(rank_ref, near_ref, mask_ref, request_ref, ghost_ref, local_ref):
    boxes = near_ref.shape[1]
    peers = request_ref.shape[0]
    part = 256
    rank = rank_ref[0]
    tri_row, tri_col = iota((part, 2 * part), 0), iota((part, 2 * part), 1)
    tri = ((tri_row < tri_col) | (tri_col >= part)).astype(F32).astype(BF16)
    peer_ids = iota((peers, part), 0)
    slot_ids = iota((CAP, part), 0)
    carry = jnp.zeros((peers, part), F32)
    sums = jnp.zeros((peers, 2 * CAP), F32)
    for side in range(2):
        for start in range(0, boxes, part):
            span = pl.ds(start, part)
            entry = near_ref[pl.ds(side, 1), span]
            live = mask_ref[:, span] > 0
            owner = lax.shift_right_arithmetic(entry, 10)
            row = lax.bitwise_and(entry, boxes - 1) + side * boxes
            mine = owner == rank
            remote = (owner >= 0) & (~mine) & live
            local_ref[pl.ds(side, 1), span] = (mine & live).astype(F32)
            target = jnp.where(remote, owner, -1)
            hot_mask = peer_ids == target
            hot_f = hot_mask.astype(F32)
            hot = hot_f.astype(BF16)
            counted = dot(hot, tri)
            before = counted[:, :part] + carry
            carry = carry + counted[:, part:]
            slot = jnp.sum(hot_f * before, axis=0, keepdims=True).astype(I32)
            ghost_ref[pl.ds(side, 1), span] = jnp.where(
                remote, owner * CAP + slot, rank * CAP
            )
            picked = slot_ids == slot
            high = lax.shift_right_logical(row, 6).astype(F32)
            low = lax.bitwise_and(row, 63).astype(F32)
            pieces = jnp.concatenate(
                [jnp.where(picked, high, 0.0), jnp.where(picked, low, 0.0)], axis=0
            )
            sums += dot(hot, pieces.astype(BF16), ((1,), (1,)))
    request = (sums[:, :CAP] * 64.0 + sums[:, CAP:]).astype(I32)
    request_ref[...] = request.reshape(peers, 1, CAP)


def route(rank, near, mask_row, peers):
    boxes = near.shape[1]
    vmem = pl.BlockSpec(memory_space=pltpu.VMEM)
    return pl.pallas_call(
        route_kernel,
        in_specs=[pl.BlockSpec(memory_space=pltpu.SMEM), vmem, vmem],
        out_specs=[vmem, vmem, vmem],
        out_shape=[
            pltpu.HBM((peers, 1, CAP), I32),
            pltpu.HBM((2, boxes), I32),
            pltpu.HBM((2, boxes), F32),
        ],
        compiler_params=LIMIT,
        name="route",
    )(rank, *in_hbm(near, mask_row))


def fill_weights(blocks_ref, weight_ref, sides):
    first_half = iota((8, LANES), 1) < SQ
    for n, side in enumerate(sides):
        for i in range(CHUNKS):
            for j in range(CHUNKS):
                def at(di, dj):
                    return blocks_ref[side, 2 * i + di, 2 * j + dj]

                k = ((n * CHUNKS + i) * CHUNKS + j) * 2
                weight_ref[k] = jnp.where(first_half, at(0, 0), at(1, 1))
                weight_ref[k + 1] = jnp.where(first_half, at(0, 1), at(1, 0))


def live_count(mask_ref, tile):
    total = jnp.int32(0)
    for family in range(TILE // 8):
        total += mask_ref[tile * TILE + family * 8]
    return total * 8


def apply_blocks(coef_ref, weight_ref, live, offset, count, put, rows=32):
    def step(r, carry):
        start = pl.multiple_of(offset + r * rows, rows)
        alive = (iota((rows, LANES), 0) + r * rows) < live
        straight, swapped = [], []
        for j in range(CHUNKS):
            x = coef_ref[pl.ds(start, rows), pl.ds(j * LANES, LANES)]
            x = jnp.where(alive, x, 0.0)
            straight.append(x.reshape(rows // 8, 8, LANES))
            swapped.append(pltpu.roll(x, SQ, 1).reshape(rows // 8, 8, LANES))
        for n in range(count):
            for i in range(CHUNKS):
                total = None
                for j in range(CHUNKS):
                    k = ((n * CHUNKS + i) * CHUNKS + j) * 2
                    term = (
                        weight_ref[k][None] * straight[j]
                        + weight_ref[k + 1][None] * swapped[j]
                    )
                    total = term if total is None else total + term
                put(n, i, start, total.reshape(rows, LANES))
        return carry

    lax.fori_loop(0, TILE // rows, step, 0)


def table_kernel(
    mask_ref, blocks_ref, coef_ref, table_ref, weight_ref, coef_vmem, table_vmem, in_sems, out_sems
):
    tiles = coef_ref.shape[0] // TILE

    def load(tile):
        span = pl.ds(pl.multiple_of(tile * TILE, TILE), TILE)
        return pltpu.make_async_copy(coef_ref.at[span], coef_vmem.at[span], in_sems.at[tile])

    def store(tile):
        span = pl.ds(pl.multiple_of(tile * TILE * CHUNKS, TILE * CHUNKS), TILE * CHUNKS)
        return pltpu.make_async_copy(
            table_vmem.at[:, span], table_ref.at[:, span], out_sems.at[tile]
        )

    for tile in range(tiles):
        load(tile).start()
    fill_weights(blocks_ref, weight_ref, (0, 2))

    def put(n, i, start, value):
        rows = value.shape[0]
        table_vmem[n, pl.ds(start * CHUNKS + i, rows, stride=CHUNKS), :] = value

    def step(tile, carry):
        load(tile).wait()
        live = live_count(mask_ref, tile)
        apply_blocks(coef_vmem, weight_ref, live, tile * TILE, 2, put)
        store(tile).start()
        return carry

    lax.fori_loop(0, tiles, step, 0)
    for tile in range(tiles):
        store(tile).wait()


def make_table(mask, blocks, coef):
    boxes = coef.shape[0]
    tiles = boxes // TILE
    return pl.pallas_call(
        table_kernel,
        in_specs=[SMEM_SPEC, SMEM_SPEC, ANYWHERE],
        out_specs=ANYWHERE,
        out_shape=pltpu.HBM((2, boxes * CHUNKS, LANES), F32),
        scratch_shapes=[
            pltpu.VMEM((2 * CHUNKS * CHUNKS * 2, 8, LANES), F32),
            pltpu.VMEM((boxes, COEFS), F32),
            pltpu.VMEM((2, boxes * CHUNKS, LANES), F32),
            pltpu.SemaphoreType.DMA((tiles,)),
            pltpu.SemaphoreType.DMA((tiles,)),
        ],
        cost_estimate=pl.CostEstimate(
            flops=boxes * COEFS * 32, bytes_accessed=boxes * COEFS * 12, transcendentals=0
        ),
        compiler_params=LIMIT,
        name="table",
    )(*in_hbm(mask, blocks, coef))


def serve_kernel(rank_ref, request_ref, table_ref, reply_ref, reply_vmem, sems):
    peers = request_ref.shape[0]
    parts = sems.shape[0]
    part = peers // parts

    def store(n):
        span = pl.ds(n * part * CAP, part * CAP)
        return pltpu.make_async_copy(reply_vmem.at[span], reply_ref.at[span], sems.at[n])

    for n in range(parts):

        def step(p, carry):
            peer = n * part + p
            for s in range(CAP):
                reply_vmem[peer * CAP + s] = table_ref[request_ref[peer, 0, s]]
            return carry

        lax.fori_loop(0, part, step, 0, unroll=True)
        own = rank_ref[0]

        @pl.when((own >= n * part) & (own < (n + 1) * part))
        def _():
            reply_vmem[pl.ds(own * CAP, CAP)] = jnp.zeros((CAP, CHUNKS, LANES), F32)

        store(n).start()
    for n in range(parts):
        store(n).wait()


def serve(rank, request, table):
    rows = request.shape[0] * CAP
    parts = 4
    return pl.pallas_call(
        serve_kernel,
        in_specs=[SMEM_SPEC, SMEM_SPEC, VMEM_SPEC],
        out_specs=ANYWHERE,
        out_shape=pltpu.HBM((rows, CHUNKS, LANES), F32),
        scratch_shapes=[
            pltpu.VMEM((rows, CHUNKS, LANES), F32),
            pltpu.SemaphoreType.DMA((parts,)),
        ],
        compiler_params=LIMIT,
        name="serve",
    )(rank, request, *in_hbm(table))


def expand(scale, rows, cols, row_of, col_of):
    pick_row = (iota((rows, 16), 1) == row_of(iota((rows, 16), 0))).astype(F32)
    pick_col = (iota((16, cols), 0) == col_of(iota((16, cols), 1))).astype(F32)
    highest = lax.Precision.HIGHEST
    wide = jnp.dot(pick_row, scale, precision=highest, preferred_element_type=F32)
    return jnp.dot(wide, pick_col, precision=highest, preferred_element_type=F32)


def base_kernel(
    mask_ref, blocks_ref, local_ref, coef_ref, table_ref, scale_ref,
    base_ref, matrix_ref, weight_ref,
):
    tile = pl.program_id(0)
    tiles = pl.num_programs(0)
    span = 2 * SQ * 2

    @pl.when(tile == 0)
    def _():
        fill_weights(blocks_ref, weight_ref, (1,))
        scale = scale_ref[...]
        scale_t = scale.T
        def bits(v, shift, mask):
            return lax.bitwise_and(lax.shift_right_logical(v, shift), mask)

        def y_of(v):
            return bits(v, 7, 1) * 8 + bits(v, 3, 7)

        def z_of(v):
            return bits(v, 6, 1) * 8 + bits(v, 0, 7)

        yz = expand(scale_t, span, span, y_of, y_of) * expand(scale_t, span, span, z_of, z_of)
        matrix_ref[0], matrix_ref[1] = split(yz)

        def x_of(v):
            return lax.shift_right_logical(v, 4)

        wide = expand(scale, span, span, x_of, x_of)
        same = bits(iota((span, span), 0), 0, 15) == bits(iota((span, span), 1), 0, 15)
        matrix_ref[2], matrix_ref[3] = split(jnp.where(same, wide, 0.0))

    def put(n, i, start, value):
        rows = value.shape[0]
        base_ref[pl.ds(start * CHUNKS + i, rows, stride=CHUNKS), :] = value

    apply_blocks(coef_ref, weight_ref, live_count(mask_ref, tile), 0, 1, put)
    boxes = tiles * TILE

    def add(b, carry):
        box = tile * TILE + b
        spot = pl.ds(b * CHUNKS, CHUNKS)
        left = table_ref[0, pl.ds(jnp.maximum(box - 1, 0) * CHUNKS, CHUNKS), :]
        right = table_ref[1, pl.ds(jnp.minimum(box + 1, boxes - 1) * CHUNKS, CHUNKS), :]
        base_ref[spot, :] += left * local_ref[0, box] + right * local_ref[1, box]
        return carry

    lax.fori_loop(0, TILE, add, 0, unroll=8)


def make_base(mask, blocks, local, coef, table, scale):
    boxes = coef.shape[0]
    span = 4 * SQ
    smem = pl.BlockSpec(memory_space=pltpu.SMEM)
    vmem = pl.BlockSpec(memory_space=pltpu.VMEM)
    return pl.pallas_call(
        base_kernel,
        grid=(boxes // TILE,),
        in_specs=[
            smem, smem, smem,
            pl.BlockSpec((TILE, COEFS), lambda t: (t, 0)),
            vmem, vmem,
        ],
        out_specs=[pl.BlockSpec((TILE * CHUNKS, LANES), lambda t: (t, 0)), vmem],
        out_shape=[pltpu.HBM((boxes * CHUNKS, LANES), F32), pltpu.HBM((4, span, span), BF16)],
        scratch_shapes=[pltpu.VMEM((CHUNKS * CHUNKS * 2, 8, LANES), F32)],
        cost_estimate=pl.CostEstimate(
            flops=boxes * COEFS * 32, bytes_accessed=boxes * COEFS * 16, transcendentals=0
        ),
        compiler_params=LIMIT,
        name="base",
    )(*in_hbm(mask, blocks, local, coef, table, scale))


def product(left, right):
    left_high, left_low = left
    right_high, right_low = right
    return (
        dot(left_high, right_high) + dot(left_low, right_high) + dot(left_high, right_low)
    )


def final_kernel(
    ghost_index_ref, ghosts_ref, base_ref, matrix_ref, wavelet_ref, derivative_ref,
    index_smem, base_vmem, rows_ref, matrix_vmem, in_high_ref, in_low_ref, out_ref,
    derivative_vmem, wavelet_vmem, index_sem, base_sem, matrix_sem, derivative_sems, wavelet_sems,
):
    families = TILE // 8
    tiles = derivative_vmem.shape[0] // TILE
    first_half = iota((families, LANES), 1) < SQ

    def derivative_copy(tile):
        span = pl.ds(tile * TILE, TILE)
        return pltpu.make_async_copy(
            derivative_vmem.at[span], derivative_ref.at[span], derivative_sems.at[tile]
        )

    def wavelet_copy(tile):
        span = pl.ds(tile * TILE, TILE)
        return pltpu.make_async_copy(
            wavelet_vmem.at[span], wavelet_ref.at[span], wavelet_sems.at[tile]
        )

    def compress_tile(tile):
        first = tile * TILE
        if tile < EARLY:
            span = pl.ds(first * CHUNKS, TILE * CHUNKS)
            rows_ref[span, :] += base_vmem[span, :]
        for j in range(CHUNKS):
            derivative_vmem[pl.ds(first, TILE), pl.ds(j * LANES, LANES)] = rows_ref[
                pl.ds(first * CHUNKS + j, TILE, stride=CHUNKS), :
            ]
        derivative_copy(tile).start()
        for cx in range(2):
            for j in range(CHUNKS):
                for cy in range(2):
                    box = first + cx * 4 + cy * 2
                    z0 = rows_ref[pl.ds(box * CHUNKS + j, families, stride=8 * CHUNKS), :]
                    z1 = rows_ref[pl.ds((box + 1) * CHUNKS + j, families, stride=8 * CHUNKS), :]
                    even = jnp.where(first_half, z0, pltpu.roll(z1, SQ, 1))
                    odd = jnp.where(first_half, pltpu.roll(z0, SQ, 1), z1)
                    for half, value in enumerate((even, odd)):
                        spot = pl.ds((cx * 8 + 2 * j + half) * families, families)
                        lanes = pl.ds(cy * LANES, LANES)
                        high, low = split(value)
                        in_high_ref[spot, lanes] = high
                        in_low_ref[spot, lanes] = low
        middle = product(
            (in_high_ref[...], in_low_ref[...]), (matrix_vmem[0], matrix_vmem[1])
        )
        result = product((matrix_vmem[2], matrix_vmem[3]), split(middle))
        for ox in range(2):
            for i in range(CHUNKS):
                for oy in range(2):
                    top = (ox * 8 + 2 * i) * families
                    lanes = slice(oy * LANES, (oy + 1) * LANES)
                    even = result[top : top + families, lanes]
                    odd = result[top + families : top + 2 * families, lanes]
                    z0 = jnp.where(first_half, even, pltpu.roll(odd, SQ, 1))
                    z1 = jnp.where(first_half, pltpu.roll(even, SQ, 1), odd)
                    box = ox * 4 + oy * 2
                    out_ref[i, pl.ds(box, families, stride=8), :] = z0
                    out_ref[i, pl.ds(box + 1, families, stride=8), :] = z1
        for i in range(CHUNKS):
            wavelet_vmem[pl.ds(first, TILE), pl.ds(i * LANES, LANES)] = out_ref[i]
        wavelet_copy(tile).start()

    index_copy = pltpu.make_async_copy(ghost_index_ref, index_smem, index_sem)
    matrix_copy = pltpu.make_async_copy(matrix_ref, matrix_vmem, matrix_sem)
    base_copy = pltpu.make_async_copy(base_ref, base_vmem, base_sem)
    index_copy.start()
    base_copy.start()
    matrix_copy.start()
    index_copy.wait()
    for tile in range(tiles):
        first = tile * TILE
        for b in range(TILE):
            box = first + b
            left = ghosts_ref[index_smem[0, box]]
            right = ghosts_ref[index_smem[1, box]]
            spot = pl.ds(box * CHUNKS, CHUNKS)
            total = left + right
            if tile >= EARLY:
                total += base_vmem[spot, :]
            rows_ref[spot, :] = total
        if tile < EARLY - 1:
            continue
        if tile == EARLY - 1:
            base_copy.wait()
            matrix_copy.wait()
        for t in range(tile + 1) if tile == EARLY - 1 else (tile,):
            compress_tile(t)
    for tile in range(tiles):
        derivative_copy(tile).wait()
        wavelet_copy(tile).wait()


def finish(ghost_index, ghosts, base, matrices):
    boxes = ghost_index.shape[1]
    span = 4 * SQ
    tiles = boxes // TILE
    return pl.pallas_call(
        final_kernel,
        in_specs=[ANYWHERE, VMEM_SPEC, ANYWHERE, ANYWHERE],
        out_specs=[ANYWHERE, ANYWHERE],
        out_shape=[jax.ShapeDtypeStruct((boxes, COEFS), F32)] * 2,
        scratch_shapes=[
            pltpu.SMEM((2, boxes), I32),
            pltpu.VMEM((boxes * CHUNKS, LANES), F32),
            pltpu.VMEM((boxes * CHUNKS, LANES), F32),
            pltpu.VMEM((4, span, span), BF16),
            pltpu.VMEM((span, span), BF16),
            pltpu.VMEM((span, span), BF16),
            pltpu.VMEM((CHUNKS, TILE, LANES), F32),
            pltpu.VMEM((boxes, COEFS), F32),
            pltpu.VMEM((boxes, COEFS), F32),
            pltpu.SemaphoreType.DMA,
            pltpu.SemaphoreType.DMA,
            pltpu.SemaphoreType.DMA,
            pltpu.SemaphoreType.DMA((tiles,)),
            pltpu.SemaphoreType.DMA((tiles,)),
        ],
        name="finish",
        compiler_params=LIMIT,
    )(*in_hbm(ghost_index), pltpu.with_memory_space_constraint(ghosts, pltpu.VMEM), *in_hbm(base, matrices))


def exchange(x):
    return lax.all_to_all(x, AXES, split_axis=0, concat_axis=0, tiled=True)


def body(coef, mask, neighbours, two_scale, deriv_blocks):
    boxes = coef.shape[0]
    rank = lax.axis_index(AXES).astype(I32).reshape(1)
    peers = lax.axis_size("morton") * lax.axis_size("level")
    request, ghost_index, local = route(rank, neighbours.T, mask.reshape(1, boxes), peers)
    asked = exchange(request)
    table = make_table(mask, deriv_blocks, coef)
    reply = serve(rank, asked, table.reshape(2 * boxes, CHUNKS, LANES))
    ghosts = exchange(reply.reshape(peers, CAP * CHUNKS, LANES))
    base, matrices = make_base(mask, deriv_blocks, local, coef, table, two_scale)
    return tuple(finish(ghost_index, ghosts.reshape(-1, CHUNKS, LANES), base, matrices))


def solution(mesh):
    in_specs = (P(AXES, None), P(AXES), P(AXES, None), P(), P())
    out_specs = (P(AXES, None), P(AXES, None))
    return jax.shard_map(body, mesh=mesh, in_specs=in_specs, out_specs=out_specs, check_vma=False)
```

```python
import jax
import jax.numpy as jnp
from jax import lax
from jax.experimental import pallas as pl
from jax.experimental.pallas import tpu as pltpu
from jax.sharding import PartitionSpec as P

ORDER = 8
COEFS = 512
SQ = ORDER * ORDER
LANES = 128
CHUNKS = COEFS // LANES
TILE = 128
CAP = 8
EARLY = 4
BOUNDS = (0, 8)
AXES = ("morton", "level")
F32 = jnp.float32
BF16 = jnp.bfloat16
I32 = jnp.int32
LIMIT = pltpu.CompilerParams(vmem_limit_bytes=24 * 1024 * 1024)
ANYWHERE = pl.BlockSpec(memory_space=pl.ANY)
VMEM_SPEC = pl.BlockSpec(memory_space=pltpu.VMEM)
SMEM_SPEC = pl.BlockSpec(memory_space=pltpu.SMEM)


def in_hbm(*arrays):
    return [pltpu.with_memory_space_constraint(x, pltpu.HBM) for x in arrays]


def iota(shape, dim):
    return lax.broadcasted_iota(I32, shape, dim)


def dot(a, b, dims=((1,), (0,))):
    return lax.dot_general(a, b, (dims, ((), ())), preferred_element_type=F32)


def split(x):
    high = x.astype(BF16)
    return high, (x - high.astype(F32)).astype(BF16)


def route_kernel(near_ref, mask_ref, request_ref, ghost_ref, local_ref):
    boxes = near_ref.shape[1]
    peers = request_ref.shape[0]
    part = 256
    rank = lax.axis_index(AXES)
    tri_row, tri_col = iota((part, 2 * part), 0), iota((part, 2 * part), 1)
    tri = ((tri_row < tri_col) | (tri_col >= part)).astype(F32).astype(BF16)
    peer_ids = iota((peers, part), 0)
    slot_ids = iota((CAP, part), 0)
    carry = jnp.zeros((peers, part), F32)
    sums = jnp.zeros((peers, 2 * CAP), F32)
    for side in range(2):
        for start in range(0, boxes, part):
            span = pl.ds(start, part)
            entry = near_ref[pl.ds(side, 1), span]
            live = mask_ref[:, span] > 0
            owner = lax.shift_right_arithmetic(entry, 10)
            row = lax.bitwise_and(entry, boxes - 1) + side * boxes
            mine = owner == rank
            remote = (owner >= 0) & (~mine) & live
            local_ref[pl.ds(side, 1), span] = (mine & live).astype(F32)
            target = jnp.where(remote, owner, -1)
            hot_mask = peer_ids == target
            hot_f = hot_mask.astype(F32)
            hot = hot_f.astype(BF16)
            counted = dot(hot, tri)
            before = counted[:, :part] + carry
            carry = carry + counted[:, part:]
            slot = jnp.sum(hot_f * before, axis=0, keepdims=True).astype(I32)
            ghost_ref[pl.ds(side, 1), span] = jnp.where(
                remote, owner * CAP + slot, rank * CAP
            )
            picked = slot_ids == slot
            high = lax.shift_right_logical(row, 6).astype(F32)
            low = lax.bitwise_and(row, 63).astype(F32)
            pieces = jnp.concatenate(
                [jnp.where(picked, high, 0.0), jnp.where(picked, low, 0.0)], axis=0
            )
            sums += dot(hot, pieces.astype(BF16), ((1,), (1,)))
    request = (sums[:, :CAP] * 64.0 + sums[:, CAP:]).astype(I32)
    request_ref[...] = request.reshape(peers, 1, CAP)


def route(near, mask_row, peers):
    boxes = near.shape[1]
    vmem = pl.BlockSpec(memory_space=pltpu.VMEM)
    return pl.pallas_call(
        route_kernel,
        in_specs=[vmem, vmem],
        out_specs=[vmem, vmem, vmem],
        out_shape=[
            pltpu.HBM((peers, 1, CAP), I32),
            pltpu.HBM((2, boxes), I32),
            pltpu.HBM((2, boxes), F32),
        ],
        compiler_params=LIMIT,
        name="route",
    )(*in_hbm(near, mask_row))


def fill_weights(blocks_ref, weight_ref, sides):
    first_half = iota((8, LANES), 1) < SQ
    for n, side in enumerate(sides):
        for i in range(CHUNKS):
            for j in range(CHUNKS):
                def at(di, dj):
                    return blocks_ref[side, 2 * i + di, 2 * j + dj]

                k = ((n * CHUNKS + i) * CHUNKS + j) * 2
                weight_ref[k] = jnp.where(first_half, at(0, 0), at(1, 1))
                weight_ref[k + 1] = jnp.where(first_half, at(0, 1), at(1, 0))


def live_count(mask_ref, tile):
    total = jnp.int32(0)
    for family in range(TILE // 8):
        total += mask_ref[tile * TILE + family * 8]
    return total * 8


def apply_blocks(coef_ref, weight_ref, live, offset, count, put, rows=32):
    def step(r, carry):
        start = pl.multiple_of(offset + r * rows, rows)
        alive = (iota((rows, LANES), 0) + r * rows) < live
        straight, swapped = [], []
        for j in range(CHUNKS):
            x = coef_ref[pl.ds(start, rows), pl.ds(j * LANES, LANES)]
            x = jnp.where(alive, x, 0.0)
            straight.append(x.reshape(rows // 8, 8, LANES))
            swapped.append(pltpu.roll(x, SQ, 1).reshape(rows // 8, 8, LANES))
        for n in range(count):
            for i in range(CHUNKS):
                total = None
                for j in range(CHUNKS):
                    k = ((n * CHUNKS + i) * CHUNKS + j) * 2
                    term = (
                        weight_ref[k][None] * straight[j]
                        + weight_ref[k + 1][None] * swapped[j]
                    )
                    total = term if total is None else total + term
                put(n, i, start, total.reshape(rows, LANES))
        return carry

    lax.fori_loop(0, TILE // rows, step, 0, unroll=True)


def table_kernel(
    mask_ref, blocks_ref, coef_ref, table_ref,
    mask_smem, blocks_smem, weight_ref, coef_vmem, table_vmem, small_sems, in_sems, out_sems,
):
    tiles = coef_ref.shape[0] // TILE

    def load(tile):
        span = pl.ds(pl.multiple_of(tile * TILE, TILE), TILE)
        return pltpu.make_async_copy(coef_ref.at[span], coef_vmem.at[span], in_sems.at[tile])

    def store(tile):
        span = pl.ds(pl.multiple_of(tile * TILE * CHUNKS, TILE * CHUNKS), TILE * CHUNKS)
        return pltpu.make_async_copy(
            table_vmem.at[:, span], table_ref.at[:, span], out_sems.at[tile]
        )

    blocks_copy = pltpu.make_async_copy(blocks_ref, blocks_smem, small_sems.at[0])
    mask_copy = pltpu.make_async_copy(mask_ref, mask_smem, small_sems.at[1])
    blocks_copy.start()
    mask_copy.start()
    for tile in range(tiles):
        load(tile).start()
    blocks_copy.wait()
    fill_weights(blocks_smem, weight_ref, (0, 2))
    mask_copy.wait()

    def put(n, i, start, value):
        rows = value.shape[0]
        table_vmem[n, pl.ds(start * CHUNKS + i, rows, stride=CHUNKS), :] = value

    def step(tile, carry):
        load(tile).wait()
        live = live_count(mask_smem, tile)
        apply_blocks(coef_vmem, weight_ref, live, tile * TILE, 2, put)
        store(tile).start()
        return carry

    lax.fori_loop(0, tiles, step, 0)
    for tile in range(tiles):
        store(tile).wait()


def make_table(mask, blocks, coef):
    boxes = coef.shape[0]
    tiles = boxes // TILE
    return pl.pallas_call(
        table_kernel,
        in_specs=[ANYWHERE, ANYWHERE, ANYWHERE],
        out_specs=ANYWHERE,
        out_shape=pltpu.HBM((2, boxes * CHUNKS, LANES), F32),
        scratch_shapes=[
            pltpu.SMEM(mask.shape, I32),
            pltpu.SMEM(blocks.shape, F32),
            pltpu.VMEM((2 * CHUNKS * CHUNKS * 2, 8, LANES), F32),
            pltpu.VMEM((boxes, COEFS), F32),
            pltpu.VMEM((2, boxes * CHUNKS, LANES), F32),
            pltpu.SemaphoreType.DMA((2,)),
            pltpu.SemaphoreType.DMA((tiles,)),
            pltpu.SemaphoreType.DMA((tiles,)),
        ],
        cost_estimate=pl.CostEstimate(
            flops=boxes * COEFS * 32, bytes_accessed=boxes * COEFS * 12, transcendentals=0
        ),
        compiler_params=LIMIT,
        name="table",
    )(*in_hbm(mask, blocks, coef))


def serve_kernel(
    request_hbm, table_hbm, reply_ref, request_ref, table_ref, reply_vmem, in_sems, sems
):
    request_copy = pltpu.make_async_copy(request_hbm, request_ref, in_sems.at[0])
    table_copy = pltpu.make_async_copy(table_hbm, table_ref, in_sems.at[1])
    request_copy.start()
    table_copy.start()
    request_copy.wait()
    table_copy.wait()
    peers = request_ref.shape[0]
    own = lax.axis_index(AXES)
    parts = sems.shape[0]
    part = peers // parts

    def store(n):
        span = pl.ds(n * part * CAP, part * CAP)
        return pltpu.make_async_copy(reply_vmem.at[span], reply_ref.at[span], sems.at[n])

    for n in range(parts):

        def step(p, carry):
            peer = n * part + p
            for s in range(CAP):
                reply_vmem[peer * CAP + s] = table_ref[request_ref[peer, 0, s]]
            return carry

        lax.fori_loop(0, part, step, 0, unroll=True)

        @pl.when((own >= n * part) & (own < (n + 1) * part))
        def _():
            reply_vmem[pl.ds(own * CAP, CAP)] = jnp.zeros((CAP, CHUNKS, LANES), F32)

        store(n).start()
    for n in range(parts):
        store(n).wait()


def serve(request, table):
    rows = request.shape[0] * CAP
    parts = 4
    return pl.pallas_call(
        serve_kernel,
        in_specs=[ANYWHERE, ANYWHERE],
        out_specs=ANYWHERE,
        out_shape=pltpu.HBM((rows, CHUNKS, LANES), F32),
        scratch_shapes=[
            pltpu.SMEM(request.shape, I32),
            pltpu.VMEM(table.shape, F32),
            pltpu.VMEM((rows, CHUNKS, LANES), F32),
            pltpu.SemaphoreType.DMA((2,)),
            pltpu.SemaphoreType.DMA((parts,)),
        ],
        compiler_params=LIMIT,
        name="serve",
    )(request, *in_hbm(table))


def expand(scale, rows, cols, row_of, col_of):
    pick_row = (iota((rows, 16), 1) == row_of(iota((rows, 16), 0))).astype(F32)
    pick_col = (iota((16, cols), 0) == col_of(iota((16, cols), 1))).astype(F32)
    highest = lax.Precision.HIGHEST
    wide = jnp.dot(pick_row, scale, precision=highest, preferred_element_type=F32)
    return jnp.dot(wide, pick_col, precision=highest, preferred_element_type=F32)


def base_kernel(
    mask_ref, blocks_ref, local_ref, coef_ref, table_ref, scale_ref,
    base_ref, matrix_ref, weight_ref,
):
    tile = pl.program_id(0)
    tiles = pl.num_programs(0)
    span = 2 * SQ * 2

    @pl.when(tile == 0)
    def _():
        fill_weights(blocks_ref, weight_ref, (1,))
        scale = scale_ref[...]
        scale_t = scale.T
        def bits(v, shift, mask):
            return lax.bitwise_and(lax.shift_right_logical(v, shift), mask)

        def y_of(v):
            return bits(v, 7, 1) * 8 + bits(v, 3, 7)

        def z_of(v):
            return bits(v, 6, 1) * 8 + bits(v, 0, 7)

        yz = expand(scale_t, span, span, y_of, y_of) * expand(scale_t, span, span, z_of, z_of)
        matrix_ref[0], matrix_ref[1] = split(yz)

        def x_of(v):
            return lax.shift_right_logical(v, 4)

        wide = expand(scale, span, span, x_of, x_of)
        same = bits(iota((span, span), 0), 0, 15) == bits(iota((span, span), 1), 0, 15)
        matrix_ref[2], matrix_ref[3] = split(jnp.where(same, wide, 0.0))

    def put(n, i, start, value):
        rows = value.shape[0]
        base_ref[pl.ds(start * CHUNKS + i, rows, stride=CHUNKS), :] = value

    apply_blocks(coef_ref, weight_ref, live_count(mask_ref, tile), 0, 1, put)
    boxes = tiles * TILE

    def add(b, carry):
        box = tile * TILE + b
        spot = pl.ds(b * CHUNKS, CHUNKS)
        left = table_ref[0, pl.ds(jnp.maximum(box - 1, 0) * CHUNKS, CHUNKS), :]
        right = table_ref[1, pl.ds(jnp.minimum(box + 1, boxes - 1) * CHUNKS, CHUNKS), :]
        base_ref[spot, :] += left * local_ref[0, box] + right * local_ref[1, box]
        return carry

    lax.fori_loop(0, TILE, add, 0, unroll=8)


def make_base(mask, blocks, local, coef, table, scale):
    boxes = coef.shape[0]
    span = 4 * SQ
    smem = pl.BlockSpec(memory_space=pltpu.SMEM)
    vmem = pl.BlockSpec(memory_space=pltpu.VMEM)
    return pl.pallas_call(
        base_kernel,
        grid=(boxes // TILE,),
        in_specs=[
            smem, smem, smem,
            pl.BlockSpec((TILE, COEFS), lambda t: (t, 0)),
            vmem, vmem,
        ],
        out_specs=[pl.BlockSpec((TILE * CHUNKS, LANES), lambda t: (t, 0)), vmem],
        out_shape=[pltpu.HBM((boxes * CHUNKS, LANES), F32), pltpu.HBM((4, span, span), BF16)],
        scratch_shapes=[pltpu.VMEM((CHUNKS * CHUNKS * 2, 8, LANES), F32)],
        cost_estimate=pl.CostEstimate(
            flops=boxes * COEFS * 32, bytes_accessed=boxes * COEFS * 16, transcendentals=0
        ),
        compiler_params=LIMIT,
        name="base",
    )(*in_hbm(mask, blocks, local, coef, table, scale))


def product(left, right):
    left_high, left_low = left
    right_high, right_low = right
    return (
        dot(left_high, right_high) + dot(left_low, right_high) + dot(left_high, right_low)
    )


def final_kernel(
    ghost_index_ref, ghosts_ref, base_ref, matrix_ref, wavelet_ref, derivative_ref,
    index_smem, base_vmem, rows_ref, matrix_vmem, in_high_ref, in_low_ref, out_ref,
    derivative_vmem, wavelet_vmem, index_sem, base_sems, matrix_sem, derivative_sems, wavelet_sems,
):
    families = TILE // 8
    tiles = derivative_vmem.shape[0] // TILE
    first_half = iota((families, LANES), 1) < SQ

    def derivative_copy(tile):
        span = pl.ds(tile * TILE, TILE)
        return pltpu.make_async_copy(
            derivative_vmem.at[span], derivative_ref.at[span], derivative_sems.at[tile]
        )

    def wavelet_copy(tile):
        span = pl.ds(tile * TILE, TILE)
        return pltpu.make_async_copy(
            wavelet_vmem.at[span], wavelet_ref.at[span], wavelet_sems.at[tile]
        )

    def compress_tile(tile):
        first = tile * TILE
        if tile < EARLY:
            span = pl.ds(first * CHUNKS, TILE * CHUNKS)
            rows_ref[span, :] += base_vmem[span, :]
        for j in range(CHUNKS):
            derivative_vmem[pl.ds(first, TILE), pl.ds(j * LANES, LANES)] = rows_ref[
                pl.ds(first * CHUNKS + j, TILE, stride=CHUNKS), :
            ]
        derivative_copy(tile).start()
        for cx in range(2):
            for j in range(CHUNKS):
                for cy in range(2):
                    box = first + cx * 4 + cy * 2
                    z0 = rows_ref[pl.ds(box * CHUNKS + j, families, stride=8 * CHUNKS), :]
                    z1 = rows_ref[pl.ds((box + 1) * CHUNKS + j, families, stride=8 * CHUNKS), :]
                    even = jnp.where(first_half, z0, pltpu.roll(z1, SQ, 1))
                    odd = jnp.where(first_half, pltpu.roll(z0, SQ, 1), z1)
                    for half, value in enumerate((even, odd)):
                        spot = pl.ds((cx * 8 + 2 * j + half) * families, families)
                        lanes = pl.ds(cy * LANES, LANES)
                        high, low = split(value)
                        in_high_ref[spot, lanes] = high
                        in_low_ref[spot, lanes] = low
        middle = product(
            (in_high_ref[...], in_low_ref[...]), (matrix_vmem[0], matrix_vmem[1])
        )
        result = product((matrix_vmem[2], matrix_vmem[3]), split(middle))
        for ox in range(2):
            for i in range(CHUNKS):
                for oy in range(2):
                    top = (ox * 8 + 2 * i) * families
                    lanes = slice(oy * LANES, (oy + 1) * LANES)
                    even = result[top : top + families, lanes]
                    odd = result[top + families : top + 2 * families, lanes]
                    z0 = jnp.where(first_half, even, pltpu.roll(odd, SQ, 1))
                    z1 = jnp.where(first_half, pltpu.roll(even, SQ, 1), odd)
                    box = ox * 4 + oy * 2
                    out_ref[i, pl.ds(box, families, stride=8), :] = z0
                    out_ref[i, pl.ds(box + 1, families, stride=8), :] = z1
        for i in range(CHUNKS):
            wavelet_vmem[pl.ds(first, TILE), pl.ds(i * LANES, LANES)] = out_ref[i]
        wavelet_copy(tile).start()

    def base_copy(n):
        span = pl.ds(BOUNDS[n] * TILE * CHUNKS, (BOUNDS[n + 1] - BOUNDS[n]) * TILE * CHUNKS)
        return pltpu.make_async_copy(base_ref.at[span], base_vmem.at[span], base_sems.at[n])

    def gather(tile, with_base):
        for box in range(tile * TILE, (tile + 1) * TILE):
            left = ghosts_ref[index_smem[0, box]]
            right = ghosts_ref[index_smem[1, box]]
            spot = pl.ds(box * CHUNKS, CHUNKS)
            total = left + right
            if with_base:
                total += base_vmem[spot, :]
            rows_ref[spot, :] = total

    index_copy = pltpu.make_async_copy(ghost_index_ref, index_smem, index_sem)
    matrix_copy = pltpu.make_async_copy(matrix_ref, matrix_vmem, matrix_sem)
    index_copy.start()
    base_copy(0).start()
    matrix_copy.start()
    for n in range(1, len(BOUNDS) - 1):
        base_copy(n).start()
    index_copy.wait()
    for tile in range(EARLY):
        gather(tile, False)
    for n in range(len(BOUNDS) - 1):
        base_copy(n).wait()
        if n == 0:
            matrix_copy.wait()
        for tile in range(BOUNDS[n], BOUNDS[n + 1]):
            if tile >= EARLY:
                gather(tile, True)
            compress_tile(tile)
    for tile in range(tiles):
        derivative_copy(tile).wait()
        wavelet_copy(tile).wait()


def finish(ghost_index, ghosts, base, matrices):
    boxes = ghost_index.shape[1]
    span = 4 * SQ
    tiles = boxes // TILE
    return pl.pallas_call(
        final_kernel,
        in_specs=[ANYWHERE, VMEM_SPEC, ANYWHERE, ANYWHERE],
        out_specs=[ANYWHERE, ANYWHERE],
        out_shape=[jax.ShapeDtypeStruct((boxes, COEFS), F32)] * 2,
        scratch_shapes=[
            pltpu.SMEM((2, boxes), I32),
            pltpu.VMEM((boxes * CHUNKS, LANES), F32),
            pltpu.VMEM((boxes * CHUNKS, LANES), F32),
            pltpu.VMEM((4, span, span), BF16),
            pltpu.VMEM((span, span), BF16),
            pltpu.VMEM((span, span), BF16),
            pltpu.VMEM((CHUNKS, TILE, LANES), F32),
            pltpu.VMEM((boxes, COEFS), F32),
            pltpu.VMEM((boxes, COEFS), F32),
            pltpu.SemaphoreType.DMA,
            pltpu.SemaphoreType.DMA((len(BOUNDS) - 1,)),
            pltpu.SemaphoreType.DMA,
            pltpu.SemaphoreType.DMA((tiles,)),
            pltpu.SemaphoreType.DMA((tiles,)),
        ],
        name="finish",
        compiler_params=LIMIT,
    )(*in_hbm(ghost_index), pltpu.with_memory_space_constraint(ghosts, pltpu.VMEM), *in_hbm(base, matrices))


def exchange(x):
    return lax.all_to_all(x, AXES, split_axis=0, concat_axis=0, tiled=True)


def body(coef, mask, neighbours, two_scale, deriv_blocks):
    boxes = coef.shape[0]
    peers = lax.axis_size("morton") * lax.axis_size("level")
    request, ghost_index, local = route(neighbours.T, mask.reshape(1, boxes), peers)
    asked = exchange(request)
    table = make_table(mask, deriv_blocks, coef)
    reply = serve(asked, table.reshape(2 * boxes, CHUNKS, LANES))
    ghosts = exchange(reply.reshape(peers, CAP * CHUNKS, LANES))
    base, matrices = make_base(mask, deriv_blocks, local, coef, table, two_scale)
    return tuple(finish(ghost_index, ghosts.reshape(-1, CHUNKS, LANES), base, matrices))


def solution(mesh):
    in_specs = (P(AXES, None), P(AXES), P(AXES, None), P(), P())
    out_specs = (P(AXES, None), P(AXES, None))
    return jax.shard_map(body, mesh=mesh, in_specs=in_specs, out_specs=out_specs, check_vma=False)
```

```python
import jax
import jax.numpy as jnp
from jax import lax
from jax.experimental import pallas as pl
from jax.experimental.pallas import tpu as pltpu
from jax.sharding import PartitionSpec as P

ORDER = 8
COEFS = 512
SQ = ORDER * ORDER
LANES = 128
CHUNKS = COEFS // LANES
TILE = 128
CAP = 8
EARLY = 4
BOUNDS = (0, 8)
AXES = ("morton", "level")
F32 = jnp.float32
BF16 = jnp.bfloat16
I32 = jnp.int32
LIMIT = pltpu.CompilerParams(vmem_limit_bytes=24 * 1024 * 1024)
ANYWHERE = pl.BlockSpec(memory_space=pl.ANY)
VMEM_SPEC = pl.BlockSpec(memory_space=pltpu.VMEM)
SMEM_SPEC = pl.BlockSpec(memory_space=pltpu.SMEM)


def in_hbm(*arrays):
    return [pltpu.with_memory_space_constraint(x, pltpu.HBM) for x in arrays]


def iota(shape, dim):
    return lax.broadcasted_iota(I32, shape, dim)


def dot(a, b, dims=((1,), (0,))):
    return lax.dot_general(a, b, (dims, ((), ())), preferred_element_type=F32)


def split(x):
    high = x.astype(BF16)
    return high, (x - high.astype(F32)).astype(BF16)


def route_kernel(near_ref, mask_ref, request_ref, ghost_ref, local_ref):
    boxes = near_ref.shape[1]
    peers = request_ref.shape[0]
    part = 256
    rank = lax.axis_index(AXES)
    tri_row, tri_col = iota((part, 2 * part), 0), iota((part, 2 * part), 1)
    tri = ((tri_row < tri_col) | (tri_col >= part)).astype(F32).astype(BF16)
    peer_ids = iota((peers, part), 0)
    slot_ids = iota((CAP, part), 0)
    carry = jnp.zeros((peers, part), F32)
    sums = jnp.zeros((peers, 2 * CAP), F32)
    for side in range(2):
        for start in range(0, boxes, part):
            span = pl.ds(start, part)
            entry = near_ref[pl.ds(side, 1), span]
            live = mask_ref[:, span] > 0
            owner = lax.shift_right_arithmetic(entry, 10)
            row = lax.bitwise_and(entry, boxes - 1) + side * boxes
            mine = owner == rank
            remote = (owner >= 0) & (~mine) & live
            local_ref[pl.ds(side, 1), span] = (mine & live).astype(F32)
            target = jnp.where(remote, owner, -1)
            hot_mask = peer_ids == target
            hot_f = hot_mask.astype(F32)
            hot = hot_f.astype(BF16)
            counted = dot(hot, tri)
            before = counted[:, :part] + carry
            carry = carry + counted[:, part:]
            slot = jnp.sum(hot_f * before, axis=0, keepdims=True).astype(I32)
            ghost_ref[pl.ds(side, 1), span] = jnp.where(
                remote, owner * CAP + slot, rank * CAP
            )
            picked = slot_ids == slot
            high = lax.shift_right_logical(row, 6).astype(F32)
            low = lax.bitwise_and(row, 63).astype(F32)
            pieces = jnp.concatenate(
                [jnp.where(picked, high, 0.0), jnp.where(picked, low, 0.0)], axis=0
            )
            sums += dot(hot, pieces.astype(BF16), ((1,), (1,)))
    request = (sums[:, :CAP] * 64.0 + sums[:, CAP:]).astype(I32)
    request_ref[...] = request.reshape(peers, 1, CAP)


def route(near, mask_row, peers):
    boxes = near.shape[1]
    vmem = pl.BlockSpec(memory_space=pltpu.VMEM)
    return pl.pallas_call(
        route_kernel,
        in_specs=[vmem, vmem],
        out_specs=[vmem, vmem, vmem],
        out_shape=[
            pltpu.HBM((peers, 1, CAP), I32),
            pltpu.HBM((2, boxes), I32),
            pltpu.HBM((2, boxes), F32),
        ],
        compiler_params=LIMIT,
        name="route",
    )(*in_hbm(near, mask_row))


def fill_weights(blocks_ref, weight_ref, sides):
    first_half = iota((8, LANES), 1) < SQ
    for n, side in enumerate(sides):
        for i in range(CHUNKS):
            for j in range(CHUNKS):
                def at(di, dj):
                    return blocks_ref[side, 2 * i + di, 2 * j + dj]

                k = ((n * CHUNKS + i) * CHUNKS + j) * 2
                weight_ref[k] = jnp.where(first_half, at(0, 0), at(1, 1))
                weight_ref[k + 1] = jnp.where(first_half, at(0, 1), at(1, 0))


def live_count(mask_ref, tile):
    total = jnp.int32(0)
    for family in range(TILE // 8):
        total += mask_ref[tile * TILE + family * 8]
    return total * 8


def apply_blocks(coef_ref, weight_ref, live, offset, count, put, rows=32):
    def step(r, carry):
        start = pl.multiple_of(offset + r * rows, rows)
        if live is not None:
            alive = (iota((rows, LANES), 0) + r * rows) < live
        straight, swapped = [], []
        for j in range(CHUNKS):
            x = coef_ref[pl.ds(start, rows), pl.ds(j * LANES, LANES)]
            if live is not None:
                x = jnp.where(alive, x, 0.0)
            straight.append(x.reshape(rows // 8, 8, LANES))
            swapped.append(pltpu.roll(x, SQ, 1).reshape(rows // 8, 8, LANES))
        for n in range(count):
            for i in range(CHUNKS):
                total = None
                for j in range(CHUNKS):
                    k = ((n * CHUNKS + i) * CHUNKS + j) * 2
                    term = (
                        weight_ref[k][None] * straight[j]
                        + weight_ref[k + 1][None] * swapped[j]
                    )
                    total = term if total is None else total + term
                put(n, i, start, total.reshape(rows, LANES))
        return carry

    lax.fori_loop(0, TILE // rows, step, 0, unroll=True)


def fill_table(coef_ref, weight_ref, mask_ref, table_ref):
    boxes = coef_ref.shape[0]

    def put(n, i, start, value):
        first = n * boxes * CHUNKS + i
        table_ref[pl.ds(start * CHUNKS + first, value.shape[0], stride=CHUNKS), :] = value

    def step(tile, carry):
        live = None if mask_ref is None else live_count(mask_ref, tile)
        apply_blocks(coef_ref, weight_ref, live, tile * TILE, 2, put)
        return carry

    lax.fori_loop(0, boxes // TILE, step, 0, unroll=mask_ref is None)


def prepare_kernel(
    mask_ref, blocks_ref, coef_ref, live_ref, weight_ref, mask_smem, blocks_smem, small_sems, sems
):
    tiles = sems.shape[0]

    def load(tile):
        span = pl.ds(tile * TILE, TILE)
        return pltpu.make_async_copy(coef_ref.at[span], live_ref.at[span], sems.at[tile])

    blocks_copy = pltpu.make_async_copy(blocks_ref, blocks_smem, small_sems.at[0])
    mask_copy = pltpu.make_async_copy(mask_ref, mask_smem, small_sems.at[1])
    blocks_copy.start()
    mask_copy.start()
    for tile in range(tiles):
        load(tile).start()
    blocks_copy.wait()
    fill_weights(blocks_smem, weight_ref, (0, 2))
    mask_copy.wait()
    half = TILE // 2
    for tile in range(tiles):
        load(tile).wait()
        alive = (iota((half, COEFS), 0) + half) < live_count(mask_smem, tile)
        span = pl.ds(tile * TILE + half, half)
        live_ref[span, :] = jnp.where(alive, live_ref[span, :], 0.0)


def prepare(mask, blocks, coef):
    boxes = coef.shape[0]
    return pl.pallas_call(
        prepare_kernel,
        in_specs=[ANYWHERE] * 3,
        out_specs=[VMEM_SPEC] * 2,
        out_shape=[
            pltpu.VMEM((boxes, COEFS), F32),
            pltpu.VMEM((2 * CHUNKS * CHUNKS * 2, 8, LANES), F32),
        ],
        scratch_shapes=[
            pltpu.SMEM(mask.shape, I32),
            pltpu.SMEM(blocks.shape, F32),
            pltpu.SemaphoreType.DMA((2,)),
            pltpu.SemaphoreType.DMA((boxes // TILE,)),
        ],
        cost_estimate=pl.CostEstimate(
            flops=boxes * COEFS * 16, bytes_accessed=boxes * COEFS * 8, transcendentals=0
        ),
        compiler_params=LIMIT,
        name="prepare",
    )(*in_hbm(mask, blocks, coef))


def serve_kernel(
    request_ref, live_ref, weight_ref, reply_ref,
    request_smem, table_vmem, reply_vmem, request_sem, out_sems,
):
    request_copy = pltpu.make_async_copy(request_ref, request_smem, request_sem)
    request_copy.start()
    fill_table(live_ref, weight_ref, None, table_vmem)
    request_copy.wait()
    peers = request_smem.shape[0]
    parts = out_sems.shape[0]
    part = peers // parts
    own = lax.axis_index(AXES)

    def store(n):
        span = pl.ds(n * part * CAP, part * CAP)
        return pltpu.make_async_copy(reply_vmem.at[span], reply_ref.at[span], out_sems.at[n])

    for n in range(parts):
        for peer in range(n * part, (n + 1) * part):
            for s in range(CAP):
                row = pl.multiple_of(request_smem[peer, 0, s] * CHUNKS, CHUNKS)
                reply_vmem[peer * CAP + s] = table_vmem[pl.ds(row, CHUNKS), :]

        @pl.when((own >= n * part) & (own < (n + 1) * part))
        def _():
            reply_vmem[pl.ds(own * CAP, CAP)] = jnp.zeros((CAP, CHUNKS, LANES), F32)

        store(n).start()
    for n in range(parts):
        store(n).wait()


def serve(request, live, weights):
    boxes = live.shape[0]
    rows = request.shape[0] * CAP
    return pl.pallas_call(
        serve_kernel,
        in_specs=[ANYWHERE, VMEM_SPEC, VMEM_SPEC],
        out_specs=ANYWHERE,
        out_shape=pltpu.HBM((rows, CHUNKS, LANES), F32),
        scratch_shapes=[
            pltpu.SMEM(request.shape, I32),
            pltpu.VMEM((2 * boxes * CHUNKS, LANES), F32),
            pltpu.VMEM((rows, CHUNKS, LANES), F32),
            pltpu.SemaphoreType.DMA,
            pltpu.SemaphoreType.DMA((4,)),
        ],
        compiler_params=LIMIT,
        name="serve",
    )(request, *[pltpu.with_memory_space_constraint(x, pltpu.VMEM) for x in (live, weights)])


def expand(scale, rows, cols, row_of, col_of):
    pick_row = (iota((rows, 16), 1) == row_of(iota((rows, 16), 0))).astype(F32)
    pick_col = (iota((16, cols), 0) == col_of(iota((16, cols), 1))).astype(F32)
    highest = lax.Precision.HIGHEST
    wide = jnp.dot(pick_row, scale, precision=highest, preferred_element_type=F32)
    return jnp.dot(wide, pick_col, precision=highest, preferred_element_type=F32)


def base_kernel(
    mask_ref, blocks_ref, local_ref, coef_ref, scale_ref,
    base_ref, matrix_ref, weight_ref, side_weight_ref, table_ref,
):
    tile = pl.program_id(0)
    tiles = pl.num_programs(0)
    span = 2 * SQ * 2

    @pl.when(tile == 0)
    def _():
        fill_weights(blocks_ref, weight_ref, (1,))
        fill_weights(blocks_ref, side_weight_ref, (0, 2))
        fill_table(coef_ref, side_weight_ref, mask_ref, table_ref)
        scale = scale_ref[...]
        scale_t = scale.T
        def bits(v, shift, mask):
            return lax.bitwise_and(lax.shift_right_logical(v, shift), mask)

        def y_of(v):
            return bits(v, 7, 1) * 8 + bits(v, 3, 7)

        def z_of(v):
            return bits(v, 6, 1) * 8 + bits(v, 0, 7)

        yz = expand(scale_t, span, span, y_of, y_of) * expand(scale_t, span, span, z_of, z_of)
        matrix_ref[0], matrix_ref[1] = split(yz)

        def x_of(v):
            return lax.shift_right_logical(v, 4)

        wide = expand(scale, span, span, x_of, x_of)
        same = bits(iota((span, span), 0), 0, 15) == bits(iota((span, span), 1), 0, 15)
        matrix_ref[2], matrix_ref[3] = split(jnp.where(same, wide, 0.0))

    def put(n, i, start, value):
        rows = value.shape[0]
        at = (start - tile * TILE) * CHUNKS + i
        base_ref[pl.ds(at, rows, stride=CHUNKS), :] = value

    apply_blocks(coef_ref, weight_ref, live_count(mask_ref, tile), tile * TILE, 1, put)
    boxes = tiles * TILE

    def add(b, carry):
        box = tile * TILE + b
        spot = pl.ds(b * CHUNKS, CHUNKS)
        left = table_ref[pl.ds(jnp.maximum(box - 1, 0) * CHUNKS, CHUNKS), :]
        right = table_ref[pl.ds((boxes + jnp.minimum(box + 1, boxes - 1)) * CHUNKS, CHUNKS), :]
        base_ref[spot, :] += left * local_ref[0, box] + right * local_ref[1, box]
        return carry

    lax.fori_loop(0, TILE, add, 0, unroll=8)


def make_base(mask, blocks, local, coef, scale):
    boxes = coef.shape[0]
    span = 4 * SQ
    smem = pl.BlockSpec(memory_space=pltpu.SMEM)
    vmem = pl.BlockSpec(memory_space=pltpu.VMEM)
    return pl.pallas_call(
        base_kernel,
        grid=(boxes // TILE,),
        in_specs=[
            smem, smem, smem,
            vmem, vmem,
        ],
        out_specs=[pl.BlockSpec((TILE * CHUNKS, LANES), lambda t: (t, 0)), vmem],
        out_shape=[pltpu.HBM((boxes * CHUNKS, LANES), F32), pltpu.HBM((4, span, span), BF16)],
        scratch_shapes=[
            pltpu.VMEM((CHUNKS * CHUNKS * 2, 8, LANES), F32),
            pltpu.VMEM((2 * CHUNKS * CHUNKS * 2, 8, LANES), F32),
            pltpu.VMEM((2 * boxes * CHUNKS, LANES), F32),
        ],
        cost_estimate=pl.CostEstimate(
            flops=boxes * COEFS * 32, bytes_accessed=boxes * COEFS * 16, transcendentals=0
        ),
        compiler_params=LIMIT,
        name="base",
    )(*in_hbm(mask, blocks, local, coef, scale))


def product(left, right):
    left_high, left_low = left
    right_high, right_low = right
    return (
        dot(left_high, right_high) + dot(left_low, right_high) + dot(left_high, right_low)
    )


def final_kernel(
    ghost_index_ref, ghosts_ref, base_ref, matrix_ref, wavelet_ref, derivative_ref,
    index_smem, base_vmem, rows_ref, matrix_vmem, in_high_ref, in_low_ref, out_ref,
    derivative_vmem, wavelet_vmem, index_sem, base_sems, matrix_sem, derivative_sems, wavelet_sems,
):
    families = TILE // 8
    tiles = derivative_vmem.shape[0] // TILE
    first_half = iota((families, LANES), 1) < SQ

    def derivative_copy(tile):
        span = pl.ds(tile * TILE, TILE)
        return pltpu.make_async_copy(
            derivative_vmem.at[span], derivative_ref.at[span], derivative_sems.at[tile]
        )

    def wavelet_copy(tile):
        span = pl.ds(tile * TILE, TILE)
        return pltpu.make_async_copy(
            wavelet_vmem.at[span], wavelet_ref.at[span], wavelet_sems.at[tile]
        )

    def compress_tile(tile):
        first = tile * TILE
        if tile < EARLY:
            span = pl.ds(first * CHUNKS, TILE * CHUNKS)
            rows_ref[span, :] += base_vmem[span, :]
        for j in range(CHUNKS):
            derivative_vmem[pl.ds(first, TILE), pl.ds(j * LANES, LANES)] = rows_ref[
                pl.ds(first * CHUNKS + j, TILE, stride=CHUNKS), :
            ]
        derivative_copy(tile).start()
        for cx in range(2):
            for j in range(CHUNKS):
                for cy in range(2):
                    box = first + cx * 4 + cy * 2
                    z0 = rows_ref[pl.ds(box * CHUNKS + j, families, stride=8 * CHUNKS), :]
                    z1 = rows_ref[pl.ds((box + 1) * CHUNKS + j, families, stride=8 * CHUNKS), :]
                    even = jnp.where(first_half, z0, pltpu.roll(z1, SQ, 1))
                    odd = jnp.where(first_half, pltpu.roll(z0, SQ, 1), z1)
                    for half, value in enumerate((even, odd)):
                        spot = pl.ds((cx * 8 + 2 * j + half) * families, families)
                        lanes = pl.ds(cy * LANES, LANES)
                        high, low = split(value)
                        in_high_ref[spot, lanes] = high
                        in_low_ref[spot, lanes] = low
        middle = product(
            (in_high_ref[...], in_low_ref[...]), (matrix_vmem[0], matrix_vmem[1])
        )
        result = product((matrix_vmem[2], matrix_vmem[3]), split(middle))
        for ox in range(2):
            for i in range(CHUNKS):
                for oy in range(2):
                    top = (ox * 8 + 2 * i) * families
                    lanes = slice(oy * LANES, (oy + 1) * LANES)
                    even = result[top : top + families, lanes]
                    odd = result[top + families : top + 2 * families, lanes]
                    z0 = jnp.where(first_half, even, pltpu.roll(odd, SQ, 1))
                    z1 = jnp.where(first_half, pltpu.roll(even, SQ, 1), odd)
                    box = ox * 4 + oy * 2
                    out_ref[i, pl.ds(box, families, stride=8), :] = z0
                    out_ref[i, pl.ds(box + 1, families, stride=8), :] = z1
        for i in range(CHUNKS):
            wavelet_vmem[pl.ds(first, TILE), pl.ds(i * LANES, LANES)] = out_ref[i]
        wavelet_copy(tile).start()

    def base_copy(n):
        span = pl.ds(BOUNDS[n] * TILE * CHUNKS, (BOUNDS[n + 1] - BOUNDS[n]) * TILE * CHUNKS)
        return pltpu.make_async_copy(base_ref.at[span], base_vmem.at[span], base_sems.at[n])

    def gather(tile, with_base):
        for box in range(tile * TILE, (tile + 1) * TILE):
            left = ghosts_ref[index_smem[0, box]]
            right = ghosts_ref[index_smem[1, box]]
            spot = pl.ds(box * CHUNKS, CHUNKS)
            total = left + right
            if with_base:
                total += base_vmem[spot, :]
            rows_ref[spot, :] = total

    index_copy = pltpu.make_async_copy(ghost_index_ref, index_smem, index_sem)
    matrix_copy = pltpu.make_async_copy(matrix_ref, matrix_vmem, matrix_sem)
    index_copy.start()
    base_copy(0).start()
    matrix_copy.start()
    for n in range(1, len(BOUNDS) - 1):
        base_copy(n).start()
    index_copy.wait()
    for tile in range(EARLY):
        gather(tile, False)
    for n in range(len(BOUNDS) - 1):
        base_copy(n).wait()
        if n == 0:
            matrix_copy.wait()
        for tile in range(BOUNDS[n], BOUNDS[n + 1]):
            if tile >= EARLY:
                gather(tile, True)
            compress_tile(tile)
    for tile in range(tiles):
        derivative_copy(tile).wait()
        wavelet_copy(tile).wait()


def finish(ghost_index, ghosts, base, matrices):
    boxes = ghost_index.shape[1]
    span = 4 * SQ
    tiles = boxes // TILE
    return pl.pallas_call(
        final_kernel,
        in_specs=[ANYWHERE, VMEM_SPEC, ANYWHERE, ANYWHERE],
        out_specs=[ANYWHERE, ANYWHERE],
        out_shape=[jax.ShapeDtypeStruct((boxes, COEFS), F32)] * 2,
        scratch_shapes=[
            pltpu.SMEM((2, boxes), I32),
            pltpu.VMEM((boxes * CHUNKS, LANES), F32),
            pltpu.VMEM((boxes * CHUNKS, LANES), F32),
            pltpu.VMEM((4, span, span), BF16),
            pltpu.VMEM((span, span), BF16),
            pltpu.VMEM((span, span), BF16),
            pltpu.VMEM((CHUNKS, TILE, LANES), F32),
            pltpu.VMEM((boxes, COEFS), F32),
            pltpu.VMEM((boxes, COEFS), F32),
            pltpu.SemaphoreType.DMA,
            pltpu.SemaphoreType.DMA((len(BOUNDS) - 1,)),
            pltpu.SemaphoreType.DMA,
            pltpu.SemaphoreType.DMA((tiles,)),
            pltpu.SemaphoreType.DMA((tiles,)),
        ],
        name="finish",
        compiler_params=LIMIT,
    )(*in_hbm(ghost_index), pltpu.with_memory_space_constraint(ghosts, pltpu.VMEM), *in_hbm(base, matrices))


def exchange(x):
    return lax.all_to_all(x, AXES, split_axis=0, concat_axis=0, tiled=True)


def body(coef, mask, neighbours, two_scale, deriv_blocks):
    boxes = coef.shape[0]
    peers = lax.axis_size("morton") * lax.axis_size("level")
    request, ghost_index, local = route(neighbours.T, mask.reshape(1, boxes), peers)
    asked = exchange(request)
    reply = serve(asked, *prepare(mask, deriv_blocks, coef))
    ghosts = exchange(reply.reshape(peers, CAP * CHUNKS, LANES))
    base, matrices = make_base(mask, deriv_blocks, local, coef, two_scale)
    return tuple(finish(ghost_index, ghosts.reshape(-1, CHUNKS, LANES), base, matrices))


def solution(mesh):
    in_specs = (P(AXES, None), P(AXES), P(AXES, None), P(), P())
    out_specs = (P(AXES, None), P(AXES, None))
    return jax.shard_map(body, mesh=mesh, in_specs=in_specs, out_specs=out_specs, check_vma=False)
```

```python
import jax
import jax.numpy as jnp
from jax import lax
from jax.experimental import pallas as pl
from jax.experimental.pallas import tpu as pltpu
from jax.sharding import PartitionSpec as P

ORDER = 8
COEFS = 512
SQ = ORDER * ORDER
LANES = 128
CHUNKS = COEFS // LANES
TILE = 128
CAP = 8
EARLY = 4
BOUNDS = (0, 8)
AXES = ("morton", "level")
F32 = jnp.float32
BF16 = jnp.bfloat16
I32 = jnp.int32
LIMIT = pltpu.CompilerParams(vmem_limit_bytes=24 * 1024 * 1024)
ANYWHERE = pl.BlockSpec(memory_space=pl.ANY)
VMEM_SPEC = pl.BlockSpec(memory_space=pltpu.VMEM)
SMEM_SPEC = pl.BlockSpec(memory_space=pltpu.SMEM)


def in_hbm(*arrays):
    return [pltpu.with_memory_space_constraint(x, pltpu.HBM) for x in arrays]


def iota(shape, dim):
    return lax.broadcasted_iota(I32, shape, dim)


def dot(a, b, dims=((1,), (0,))):
    return lax.dot_general(a, b, (dims, ((), ())), preferred_element_type=F32)


def split(x):
    high = x.astype(BF16)
    return high, (x - high.astype(F32)).astype(BF16)


def route_kernel(near_ref, mask_ref, request_ref, ghost_ref, local_ref):
    boxes = near_ref.shape[1]
    peers = request_ref.shape[0]
    part = 256
    rank = lax.axis_index(AXES)
    tri_row, tri_col = iota((part, 2 * part), 0), iota((part, 2 * part), 1)
    tri = ((tri_row < tri_col) | (tri_col >= part)).astype(F32).astype(BF16)
    peer_ids = iota((peers, part), 0)
    slot_ids = iota((CAP, part), 0)
    carry = jnp.zeros((peers, part), F32)
    sums = jnp.zeros((peers, 2 * CAP), F32)
    for side in range(2):
        for start in range(0, boxes, part):
            span = pl.ds(start, part)
            entry = near_ref[pl.ds(side, 1), span]
            live = mask_ref[:, span] > 0
            owner = lax.shift_right_arithmetic(entry, 10)
            row = lax.bitwise_and(entry, boxes - 1) + side * boxes
            mine = owner == rank
            remote = (owner >= 0) & (~mine) & live
            local_ref[pl.ds(side, 1), span] = (mine & live).astype(F32)
            target = jnp.where(remote, owner, -1)
            hot_mask = peer_ids == target
            hot_f = hot_mask.astype(F32)
            hot = hot_f.astype(BF16)
            counted = dot(hot, tri)
            before = counted[:, :part] + carry
            carry = carry + counted[:, part:]
            slot = jnp.sum(hot_f * before, axis=0, keepdims=True).astype(I32)
            ghost_ref[pl.ds(side, 1), span] = jnp.where(
                remote, owner * CAP + slot, rank * CAP
            )
            picked = slot_ids == slot
            high = lax.shift_right_logical(row, 6).astype(F32)
            low = lax.bitwise_and(row, 63).astype(F32)
            pieces = jnp.concatenate(
                [jnp.where(picked, high, 0.0), jnp.where(picked, low, 0.0)], axis=0
            )
            sums += dot(hot, pieces.astype(BF16), ((1,), (1,)))
    request = (sums[:, :CAP] * 64.0 + sums[:, CAP:]).astype(I32)
    request_ref[...] = request.reshape(peers, 1, CAP)


def route(near, mask_row, peers):
    boxes = near.shape[1]
    vmem = pl.BlockSpec(memory_space=pltpu.VMEM)
    return pl.pallas_call(
        route_kernel,
        in_specs=[vmem, vmem],
        out_specs=[vmem, vmem, vmem],
        out_shape=[
            pltpu.HBM((peers, 1, CAP), I32),
            pltpu.HBM((2, boxes), I32),
            pltpu.HBM((2, boxes), F32),
        ],
        compiler_params=LIMIT,
        name="route",
    )(*in_hbm(near, mask_row))


def fill_weights(blocks_ref, weight_ref, sides):
    first_half = iota((8, LANES), 1) < SQ
    for n, side in enumerate(sides):
        for i in range(CHUNKS):
            for j in range(CHUNKS):
                def at(di, dj):
                    return blocks_ref[side, 2 * i + di, 2 * j + dj]

                k = ((n * CHUNKS + i) * CHUNKS + j) * 2
                weight_ref[k] = jnp.where(first_half, at(0, 0), at(1, 1))
                weight_ref[k + 1] = jnp.where(first_half, at(0, 1), at(1, 0))


def live_count(mask_ref, tile):
    total = jnp.int32(0)
    for family in range(TILE // 8):
        total += mask_ref[tile * TILE + family * 8]
    return total * 8


def apply_blocks(coef_ref, weight_ref, live, offset, count, put, rows=32):
    def step(r, carry):
        start = pl.multiple_of(offset + r * rows, rows)
        if live is not None:
            alive = (iota((rows, LANES), 0) + r * rows) < live
        straight, swapped = [], []
        for j in range(CHUNKS):
            x = coef_ref[pl.ds(start, rows), pl.ds(j * LANES, LANES)]
            if live is not None:
                x = jnp.where(alive, x, 0.0)
            straight.append(x.reshape(rows // 8, 8, LANES))
            swapped.append(pltpu.roll(x, SQ, 1).reshape(rows // 8, 8, LANES))
        for n in range(count):
            for i in range(CHUNKS):
                total = None
                for j in range(CHUNKS):
                    k = ((n * CHUNKS + i) * CHUNKS + j) * 2
                    term = (
                        weight_ref[k][None] * straight[j]
                        + weight_ref[k + 1][None] * swapped[j]
                    )
                    total = term if total is None else total + term
                put(n, i, start, total.reshape(rows, LANES))
        return carry

    lax.fori_loop(0, TILE // rows, step, 0, unroll=True)


def fill_table(coef_ref, weight_ref, mask_ref, table_ref):
    boxes = coef_ref.shape[0]

    def put(n, i, start, value):
        first = n * boxes * CHUNKS + i
        table_ref[pl.ds(start * CHUNKS + first, value.shape[0], stride=CHUNKS), :] = value

    def step(tile, carry):
        live = None if mask_ref is None else live_count(mask_ref, tile)
        apply_blocks(coef_ref, weight_ref, live, tile * TILE, 2, put)
        return carry

    lax.fori_loop(0, boxes // TILE, step, 0, unroll=mask_ref is None)


def prepare_kernel(
    mask_ref, blocks_ref, coef_ref, live_ref, weight_ref, mask_smem, blocks_smem, small_sems, sems
):
    tiles = sems.shape[0]

    def load(tile):
        span = pl.ds(tile * TILE, TILE)
        return pltpu.make_async_copy(coef_ref.at[span], live_ref.at[span], sems.at[tile])

    blocks_copy = pltpu.make_async_copy(blocks_ref, blocks_smem, small_sems.at[0])
    mask_copy = pltpu.make_async_copy(mask_ref, mask_smem, small_sems.at[1])
    blocks_copy.start()
    mask_copy.start()
    for tile in range(tiles):
        load(tile).start()
    blocks_copy.wait()
    fill_weights(blocks_smem, weight_ref, (0, 2))
    mask_copy.wait()
    half = TILE // 2
    for tile in range(tiles):
        load(tile).wait()
        alive = (iota((half, COEFS), 0) + half) < live_count(mask_smem, tile)
        span = pl.ds(tile * TILE + half, half)
        live_ref[span, :] = jnp.where(alive, live_ref[span, :], 0.0)


def prepare(mask, blocks, coef):
    boxes = coef.shape[0]
    return pl.pallas_call(
        prepare_kernel,
        in_specs=[ANYWHERE] * 3,
        out_specs=[VMEM_SPEC] * 2,
        out_shape=[
            pltpu.VMEM((boxes, COEFS), F32),
            pltpu.VMEM((2 * CHUNKS * CHUNKS * 2, 8, LANES), F32),
        ],
        scratch_shapes=[
            pltpu.SMEM(mask.shape, I32),
            pltpu.SMEM(blocks.shape, F32),
            pltpu.SemaphoreType.DMA((2,)),
            pltpu.SemaphoreType.DMA((boxes // TILE,)),
        ],
        cost_estimate=pl.CostEstimate(
            flops=boxes * COEFS * 16, bytes_accessed=boxes * COEFS * 8, transcendentals=0
        ),
        compiler_params=LIMIT,
        name="prepare",
    )(*in_hbm(mask, blocks, coef))


def serve_kernel(
    request_ref, live_ref, weight_ref, reply_ref,
    request_smem, table_vmem, reply_vmem, request_sem, out_sems,
):
    request_copy = pltpu.make_async_copy(request_ref, request_smem, request_sem)
    request_copy.start()
    fill_table(live_ref, weight_ref, None, table_vmem)
    request_copy.wait()
    peers = request_smem.shape[0]
    parts = out_sems.shape[0]
    part = peers // parts
    own = lax.axis_index(AXES)

    def store(n):
        span = pl.ds(n * part * CAP, part * CAP)
        return pltpu.make_async_copy(reply_vmem.at[span], reply_ref.at[span], out_sems.at[n])

    for n in range(parts):
        for peer in range(n * part, (n + 1) * part):
            for s in range(CAP):
                row = pl.multiple_of(request_smem[peer, 0, s] * CHUNKS, CHUNKS)
                reply_vmem[peer * CAP + s] = table_vmem[pl.ds(row, CHUNKS), :]

        @pl.when((own >= n * part) & (own < (n + 1) * part))
        def _():
            reply_vmem[pl.ds(own * CAP, CAP)] = jnp.zeros((CAP, CHUNKS, LANES), F32)

        store(n).start()
    for n in range(parts):
        store(n).wait()


def serve(request, live, weights):
    boxes = live.shape[0]
    rows = request.shape[0] * CAP
    return pl.pallas_call(
        serve_kernel,
        in_specs=[ANYWHERE, VMEM_SPEC, VMEM_SPEC],
        out_specs=ANYWHERE,
        out_shape=pltpu.HBM((rows, CHUNKS, LANES), F32),
        scratch_shapes=[
            pltpu.SMEM(request.shape, I32),
            pltpu.VMEM((2 * boxes * CHUNKS, LANES), F32),
            pltpu.VMEM((rows, CHUNKS, LANES), F32),
            pltpu.SemaphoreType.DMA,
            pltpu.SemaphoreType.DMA((4,)),
        ],
        compiler_params=LIMIT,
        name="serve",
    )(request, *[pltpu.with_memory_space_constraint(x, pltpu.VMEM) for x in (live, weights)])


def expand(scale, rows, cols, row_of, col_of):
    pick_row = (iota((rows, 16), 1) == row_of(iota((rows, 16), 0))).astype(F32)
    pick_col = (iota((16, cols), 0) == col_of(iota((16, cols), 1))).astype(F32)
    highest = lax.Precision.HIGHEST
    wide = jnp.dot(pick_row, scale, precision=highest, preferred_element_type=F32)
    return jnp.dot(wide, pick_col, precision=highest, preferred_element_type=F32)


def base_kernel(
    mask_ref, blocks_ref, local_ref, coef_ref, scale_ref,
    base_ref, matrix_ref, weight_ref, side_weight_ref, table_ref,
):
    tile = pl.program_id(0)
    tiles = pl.num_programs(0)
    span = 2 * SQ * 2

    @pl.when(tile == 0)
    def _():
        fill_weights(blocks_ref, weight_ref, (1,))
        fill_weights(blocks_ref, side_weight_ref, (0, 2))
        fill_table(coef_ref, side_weight_ref, mask_ref, table_ref)
        scale = scale_ref[...]
        scale_t = scale.T
        def bits(v, shift, mask):
            return lax.bitwise_and(lax.shift_right_logical(v, shift), mask)

        def y_of(v):
            return bits(v, 7, 1) * 8 + bits(v, 3, 7)

        def z_of(v):
            return bits(v, 6, 1) * 8 + bits(v, 0, 7)

        yz = expand(scale_t, span, span, y_of, y_of) * expand(scale_t, span, span, z_of, z_of)
        matrix_ref[0], matrix_ref[1] = split(yz)

        def x_of(v):
            return lax.shift_right_logical(v, 4)

        wide = expand(scale, span, span, x_of, x_of)
        same = bits(iota((span, span), 0), 0, 15) == bits(iota((span, span), 1), 0, 15)
        matrix_ref[2], matrix_ref[3] = split(jnp.where(same, wide, 0.0))

    def put(n, i, start, value):
        rows = value.shape[0]
        at = (start - tile * TILE) * CHUNKS + i
        base_ref[pl.ds(at, rows, stride=CHUNKS), :] = value

    apply_blocks(coef_ref, weight_ref, live_count(mask_ref, tile), tile * TILE, 1, put)
    boxes = tiles * TILE

    def add(b, carry):
        box = tile * TILE + b
        spot = pl.ds(b * CHUNKS, CHUNKS)
        left = table_ref[pl.ds(jnp.maximum(box - 1, 0) * CHUNKS, CHUNKS), :]
        right = table_ref[pl.ds((boxes + jnp.minimum(box + 1, boxes - 1)) * CHUNKS, CHUNKS), :]
        base_ref[spot, :] += left * local_ref[0, box] + right * local_ref[1, box]
        return carry

    lax.fori_loop(0, TILE, add, 0, unroll=8)


def make_base(mask, blocks, local, coef, scale):
    boxes = coef.shape[0]
    span = 4 * SQ
    smem = pl.BlockSpec(memory_space=pltpu.SMEM)
    vmem = pl.BlockSpec(memory_space=pltpu.VMEM)
    return pl.pallas_call(
        base_kernel,
        grid=(boxes // TILE,),
        in_specs=[
            smem, smem, smem,
            vmem, vmem,
        ],
        out_specs=[pl.BlockSpec((TILE * CHUNKS, LANES), lambda t: (t, 0)), vmem],
        out_shape=[pltpu.HBM((boxes * CHUNKS, LANES), F32), pltpu.HBM((4, span, span), BF16)],
        scratch_shapes=[
            pltpu.VMEM((CHUNKS * CHUNKS * 2, 8, LANES), F32),
            pltpu.VMEM((2 * CHUNKS * CHUNKS * 2, 8, LANES), F32),
            pltpu.VMEM((2 * boxes * CHUNKS, LANES), F32),
        ],
        cost_estimate=pl.CostEstimate(
            flops=boxes * COEFS * 32, bytes_accessed=boxes * COEFS * 16, transcendentals=0
        ),
        compiler_params=LIMIT,
        name="base",
    )(*in_hbm(mask, blocks, local, coef, scale))


def product(left, right):
    left_high, left_low = left
    right_high, right_low = right
    return dot(
        jnp.concatenate([left_high, left_low, left_high], axis=1),
        jnp.concatenate([right_high, right_high, right_low], axis=0),
    )


def final_kernel(
    ghost_index_ref, ghosts_ref, base_ref, matrix_ref, wavelet_ref, derivative_ref,
    index_smem, base_vmem, rows_ref, matrix_vmem, in_high_ref, in_low_ref, out_ref,
    derivative_vmem, index_sem, base_sems, matrix_sem, derivative_sems, wavelet_sems,
):
    families = TILE // 8
    tiles = derivative_vmem.shape[0] // TILE
    first_half = iota((families, LANES), 1) < SQ

    def derivative_copy(tile):
        span = pl.ds(tile * TILE, TILE)
        return pltpu.make_async_copy(
            derivative_vmem.at[span], derivative_ref.at[span], derivative_sems.at[tile]
        )

    def wavelet_copy(tile, i):
        span = pl.ds(tile * TILE, TILE)
        return pltpu.make_async_copy(
            out_ref.at[i, span], wavelet_ref.at[span, pl.ds(i * LANES, LANES)], wavelet_sems.at[tile, i]
        )

    def compress_tile(tile):
        first = tile * TILE
        if tile < EARLY:
            span = pl.ds(first * CHUNKS, TILE * CHUNKS)
            rows_ref[span, :] += base_vmem[span, :]
        for j in range(CHUNKS):
            derivative_vmem[pl.ds(first, TILE), pl.ds(j * LANES, LANES)] = rows_ref[
                pl.ds(first * CHUNKS + j, TILE, stride=CHUNKS), :
            ]
        derivative_copy(tile).start()
        for cx in range(2):
            for j in range(CHUNKS):
                for cy in range(2):
                    box = first + cx * 4 + cy * 2
                    z0 = rows_ref[pl.ds(box * CHUNKS + j, families, stride=8 * CHUNKS), :]
                    z1 = rows_ref[pl.ds((box + 1) * CHUNKS + j, families, stride=8 * CHUNKS), :]
                    even = jnp.where(first_half, z0, pltpu.roll(z1, SQ, 1))
                    odd = jnp.where(first_half, pltpu.roll(z0, SQ, 1), z1)
                    for half, value in enumerate((even, odd)):
                        spot = pl.ds((cx * 8 + 2 * j + half) * families, families)
                        lanes = pl.ds(cy * LANES, LANES)
                        high, low = split(value)
                        in_high_ref[spot, lanes] = high
                        in_low_ref[spot, lanes] = low
        middle = product(
            (in_high_ref[...], in_low_ref[...]), (matrix_vmem[0], matrix_vmem[1])
        )
        result = product((matrix_vmem[2], matrix_vmem[3]), split(middle))
        for ox in range(2):
            for i in range(CHUNKS):
                for oy in range(2):
                    top = (ox * 8 + 2 * i) * families
                    lanes = slice(oy * LANES, (oy + 1) * LANES)
                    even = result[top : top + families, lanes]
                    odd = result[top + families : top + 2 * families, lanes]
                    z0 = jnp.where(first_half, even, pltpu.roll(odd, SQ, 1))
                    z1 = jnp.where(first_half, pltpu.roll(even, SQ, 1), odd)
                    box = ox * 4 + oy * 2
                    out_ref[i, pl.ds(first + box, families, stride=8), :] = z0
                    out_ref[i, pl.ds(first + box + 1, families, stride=8), :] = z1
        for i in range(CHUNKS):
            wavelet_copy(tile, i).start()

    def base_copy(n):
        span = pl.ds(BOUNDS[n] * TILE * CHUNKS, (BOUNDS[n + 1] - BOUNDS[n]) * TILE * CHUNKS)
        return pltpu.make_async_copy(base_ref.at[span], base_vmem.at[span], base_sems.at[n])

    def gather(tile, with_base):
        for box in range(tile * TILE, (tile + 1) * TILE):
            left = ghosts_ref[index_smem[0, box]]
            right = ghosts_ref[index_smem[1, box]]
            spot = pl.ds(box * CHUNKS, CHUNKS)
            total = left + right
            if with_base:
                total += base_vmem[spot, :]
            rows_ref[spot, :] = total

    index_copy = pltpu.make_async_copy(ghost_index_ref, index_smem, index_sem)
    matrix_copy = pltpu.make_async_copy(matrix_ref, matrix_vmem, matrix_sem)
    index_copy.start()
    base_copy(0).start()
    matrix_copy.start()
    for n in range(1, len(BOUNDS) - 1):
        base_copy(n).start()
    index_copy.wait()
    for tile in range(EARLY):
        gather(tile, False)
    for n in range(len(BOUNDS) - 1):
        base_copy(n).wait()
        if n == 0:
            matrix_copy.wait()
        for tile in range(BOUNDS[n], BOUNDS[n + 1]):
            if tile >= EARLY:
                gather(tile, True)
            compress_tile(tile)
    for tile in range(tiles):
        derivative_copy(tile).wait()
        for i in range(CHUNKS):
            wavelet_copy(tile, i).wait()


def finish(ghost_index, ghosts, base, matrices):
    boxes = ghost_index.shape[1]
    span = 4 * SQ
    tiles = boxes // TILE
    return pl.pallas_call(
        final_kernel,
        in_specs=[ANYWHERE, VMEM_SPEC, ANYWHERE, ANYWHERE],
        out_specs=[ANYWHERE, ANYWHERE],
        out_shape=[jax.ShapeDtypeStruct((boxes, COEFS), F32)] * 2,
        scratch_shapes=[
            pltpu.SMEM((2, boxes), I32),
            pltpu.VMEM((boxes * CHUNKS, LANES), F32),
            pltpu.VMEM((boxes * CHUNKS, LANES), F32),
            pltpu.VMEM((4, span, span), BF16),
            pltpu.VMEM((span, span), BF16),
            pltpu.VMEM((span, span), BF16),
            pltpu.VMEM((CHUNKS, boxes, LANES), F32),
            pltpu.VMEM((boxes, COEFS), F32),
            pltpu.SemaphoreType.DMA,
            pltpu.SemaphoreType.DMA((len(BOUNDS) - 1,)),
            pltpu.SemaphoreType.DMA,
            pltpu.SemaphoreType.DMA((tiles,)),
            pltpu.SemaphoreType.DMA((tiles, CHUNKS)),
        ],
        name="finish",
        compiler_params=LIMIT,
    )(*in_hbm(ghost_index), pltpu.with_memory_space_constraint(ghosts, pltpu.VMEM), *in_hbm(base, matrices))


def exchange(x):
    return lax.all_to_all(x, AXES, split_axis=0, concat_axis=0, tiled=True)


def body(coef, mask, neighbours, two_scale, deriv_blocks):
    boxes = coef.shape[0]
    peers = lax.axis_size("morton") * lax.axis_size("level")
    request, ghost_index, local = route(neighbours.T, mask.reshape(1, boxes), peers)
    asked = exchange(request)
    reply = serve(asked, *prepare(mask, deriv_blocks, coef))
    ghosts = exchange(reply.reshape(peers, CAP * CHUNKS, LANES))
    base, matrices = make_base(mask, deriv_blocks, local, coef, two_scale)
    return tuple(finish(ghost_index, ghosts.reshape(-1, CHUNKS, LANES), base, matrices))


def solution(mesh):
    in_specs = (P(AXES, None), P(AXES), P(AXES, None), P(), P())
    out_specs = (P(AXES, None), P(AXES, None))
    return jax.shard_map(body, mesh=mesh, in_specs=in_specs, out_specs=out_specs, check_vma=False)
```
